256 devices in a mesh: blk: 32 (over y_lo, z, core), rep: 8 (over x, y_hi).
Axes of the slice: x: 4, y: 4 (y_hi: 2, y_lo: 2; y = y_hi * 2 + y_lo), z: 8, core: 2. Of those that a mesh axis runs over, the one named last changes fastest.
Arguments:
- features: bfloat16 [32768, 256], P('blk'), may hold values from -6 to 6
- weight_self: bfloat16 [256, 256], replicated, may hold values from -0.375 to 0.375
- weight_neighbor: bfloat16 [256, 256], replicated, may hold values from -0.375 to 0.375
- bias_vector: float32 [256], replicated, may hold values from -3 to 3
- tile_row: int32 [32, 32, 64], P('blk', 'rep'), may hold values from 0 to 7
- tile_column: int32 [32, 32, 64], P('blk', 'rep'), may hold values from 0 to 7
- tile_value: int32 [32, 32, 64], P('blk', 'rep'), may hold values from 0 to 127
- tile_count: int32 [32, 32], P('blk', 'rep'), may hold values from 16 to 64
- tile_table: bfloat16 [32768, 128, 128], P(('blk', 'rep')), may hold values from -0.046875 to 0.046875
- cotangent: bfloat16 [32768, 256], P('blk'), may hold values from -6 to 6
Outputs:
- activations: bfloat16 [32768, 256], P('blk')
- grad_features: bfloat16 [32768, 256], P('blk')
- grad_weight_self: float32 [256, 256], replicated
- grad_weight_neighbor: float32 [256, 256], replicated
- grad_bias: float32 [256], replicated
The draws below stay inside these ranges and needn't reach their ends.
All inputs are finite; a program needn't handle non-finite values.
Results may differ from the reference program's by a relative error of at most 0.025.
Values may be sent and summed in bfloat16 or wider, within the bound.
No kernel may reach another device: no remote copies, remote signals or barrier semaphores. Data moves between devices by JAX's collectives and lax.ppermute only.
A program may use at most 64 MiB of HBM per device.

```python
import jax
import jax.numpy as jnp
from jax import lax

F = 256
TILE = 128
R_DEV = 1024
SLOTS = 64
VALS = 128
BLOCKS_DEV = 8
GROUPS = 32
STEPS = 32
NODES = 32768
TABLE_TILES = 32768
N_BLK = 32
N_REP = 8


def draw_tile_count(key, part):
    step_ids = jnp.arange(STEPS, dtype=jnp.int32)
    distance = jnp.minimum(step_ids, STEPS - step_ids)
    drawn = jax.random.randint(key, (GROUPS, STEPS), SLOTS // 4, SLOTS // 2 + 1, dtype=jnp.int32)
    return jnp.where(distance[None, :] <= 1, SLOTS, drawn).astype(jnp.int32)


def touch_ends(entries, key, low, top_value):
    extent = entries.shape
    place = [jax.random.randint(jax.random.fold_in(key, axis), (), 0, extent[axis]) for axis in range(len(extent))]
    entries = entries.at[tuple(place)].set(low)
    longest = extent.index(max(extent))
    place[longest] = (place[longest] + 1) % extent[longest]
    return entries.at[tuple(place)].set(top_value)


def steps_of(rng, extent, split, smallest, high):
    gain = 1.0
    for dim, blocks in split:
        draws = jax.random.uniform(jax.random.fold_in(jax.random.fold_in(rng, 6), dim), (blocks,), jnp.float32, smallest / len(split), high / len(split))
        gain = gain * jnp.repeat(jnp.exp(draws), extent[dim] // blocks).reshape((-1,) + (1,) * (len(extent) - 1 - dim))
    return gain


def scatter_about(own_key, extent, width, bound, pieces=(), kind=jnp.bfloat16):
    gain = steps_of(own_key, extent, pieces, -0.22, 0.18) if pieces else 1.0
    result = jax.random.normal(own_key, extent, jnp.float32) * width * gain
    return jnp.minimum(jnp.maximum(result, -bound), bound).astype(kind)


def setup_inputs(seed: int = 0) -> dict:
    streams_of = jax.random.split(jax.random.key(seed), 11)
    features = scatter_about(streams_of[0], (NODES, F), 1.0, 6.0, ((0, 32),))
    weight_self = scatter_about(streams_of[1], (F, F), F ** -0.5, 0.375)
    weight_neighbor = scatter_about(streams_of[2], (F, F), F ** -0.5, 0.375)
    bias_vector = scatter_about(streams_of[3], (F,), 0.5, 3.0, (), jnp.float32)
    tile_row = touch_ends(jax.random.randint(streams_of[4], (GROUPS, STEPS, SLOTS), 0, BLOCKS_DEV), jax.random.fold_in(streams_of[4], 1), 0, BLOCKS_DEV - 1).astype(jnp.int32)
    tile_column = touch_ends(jax.random.randint(streams_of[5], (GROUPS, STEPS, SLOTS), 0, BLOCKS_DEV), jax.random.fold_in(streams_of[5], 1), 0, BLOCKS_DEV - 1).astype(jnp.int32)
    tile_value = touch_ends(jax.random.randint(streams_of[6], (GROUPS, STEPS, SLOTS), 0, VALS), jax.random.fold_in(streams_of[6], 1), 0, VALS - 1).astype(jnp.int32)
    tile_count = draw_tile_count(jax.random.fold_in(streams_of[10], 71), 0)
    tile_table = scatter_about(streams_of[8], (TABLE_TILES, TILE, TILE), (TILE * SLOTS * STEPS * TILE // (2 * R_DEV)) ** -0.5, 0.046875, ((0, 256),))
    cotangent = scatter_about(streams_of[9], (NODES, F), 1.0, 6.0, ((0, 32),))
    return dict(features=features, weight_self=weight_self, weight_neighbor=weight_neighbor, bias_vector=bias_vector, tile_row=tile_row, tile_column=tile_column, tile_value=tile_value, tile_count=tile_count, tile_table=tile_table, cotangent=cotangent)


def reference(features, weight_self, weight_neighbor, bias_vector, tile_row, tile_column, tile_value, tile_count, tile_table, cotangent):
    block_count = R_DEV // TILE
    step_count = N_BLK // N_REP
    step_ids = jnp.arange(N_BLK, dtype=jnp.int32)
    slot_index = jnp.arange(SLOTS, dtype=jnp.int32)
    block_index = jnp.arange(block_count, dtype=jnp.int32)
    value_table = tile_table.astype(jnp.float32)
    source_blocks = features.astype(jnp.float32).reshape(N_BLK, block_count, TILE, F)

    def lists_of(group_id):
        table_base = (group_id * N_REP + step_ids // step_count) * VALS
        tile_values = value_table[table_base[:, None] + tile_value[group_id]]
        is_live = slot_index[None, :] < tile_count[group_id][:, None]
        rows_hit = ((tile_row[group_id][..., None] == block_index) & is_live[..., None]).astype(jnp.float32)
        columns_hit = ((tile_column[group_id][..., None] == block_index) & is_live[..., None]).astype(jnp.float32)
        partner = ((group_id - step_ids) % N_BLK).astype(jnp.int32)
        return tile_values, rows_hit, columns_hit, partner

    def forward_group(group_id):
        tile_values, rows_hit, columns_hit, partner = lists_of(group_id)
        picked = source_blocks[partner[:, None], tile_column[group_id]]
        products = jnp.einsum("skab,skbf->skaf", tile_values, picked)
        return jnp.einsum("skr,skaf->raf", rows_hit, products)

    aggregate = lax.map(forward_group, step_ids)
    aggregate_b = aggregate.reshape(NODES, F).astype(jnp.bfloat16)
    before = jnp.dot(features, weight_self, preferred_element_type=jnp.float32)
    before = before + jnp.dot(aggregate_b, weight_neighbor, preferred_element_type=jnp.float32) + bias_vector
    sigmoid_pre = jax.nn.sigmoid(before)
    activations = (before * sigmoid_pre).astype(jnp.bfloat16)
    derivative = sigmoid_pre * (1.0 + before * (1.0 - sigmoid_pre))
    grad_pre = (cotangent.astype(jnp.float32) * derivative).astype(jnp.bfloat16)
    grad_weight_self = jnp.dot(features.T, grad_pre, preferred_element_type=jnp.float32)
    grad_weight_neighbor = jnp.dot(aggregate_b.T, grad_pre, preferred_element_type=jnp.float32)
    grad_bias = jnp.sum(grad_pre.astype(jnp.float32), axis=0)
    self_term = jnp.dot(grad_pre, weight_self.T, preferred_element_type=jnp.float32)
    sent_back = jnp.dot(grad_pre, weight_neighbor.T, preferred_element_type=jnp.float32).astype(jnp.bfloat16)
    sent_blocks = sent_back.astype(jnp.float32).reshape(N_BLK, block_count, TILE, F)

    def backward_group(running, group_id):
        tile_values, rows_hit, columns_hit, partner = lists_of(group_id)
        picked = sent_blocks[group_id][tile_row[group_id]]
        products = jnp.einsum("skab,skaf->skbf", tile_values, picked)
        addition = jnp.einsum("skc,skbf->scbf", columns_hit, products)
        return running.at[partner].add(addition), None

    pushed, unused = lax.scan(backward_group, jnp.zeros((N_BLK, block_count, TILE, F), jnp.float32), step_ids)
    grad_features = (self_term + pushed.reshape(NODES, F)).astype(jnp.bfloat16)
    return activations, grad_features, grad_weight_self, grad_weight_neighbor, grad_bias
```

```python
import functools

import jax
import jax.numpy as jnp
from jax import lax
from jax.experimental import pallas as pl
from jax.experimental.pallas import tpu as pltpu
from jax.sharding import PartitionSpec as P

BOTH = ("blk", "rep")
CONTRACT_ROWS = (((0,), (0,)), ((), ()))
CONTRACT_COLUMNS = (((1,), (1,)), ((), ()))


def permuted(array, target):
    groups, replicas = lax.axis_size("blk"), lax.axis_size("rep")
    pairs = []
    for g in range(groups):
        for r in range(replicas):
            to_g, to_r = target(g, r)
            pairs.append((g * replicas + r, to_g % groups * replicas + to_r % replicas))
    return lax.ppermute(array, BOTH, pairs)


def build_kernel(row_ref, column_ref, value_ref, count_ref, table_ref, *refs):
    out_refs, total_ref = refs[:-1], refs[-1]
    blocks = total_ref.shape[0]
    for step, out_ref in enumerate(out_refs):
        total_ref[...] = jnp.zeros_like(total_ref)

        def add_tile(slot, unused, step=step):
            row = row_ref[step, slot]
            column = column_ref[step, slot]
            value = value_ref[step, slot]
            total_ref[row, column] += table_ref[value].astype(jnp.float32)
            return unused

        lax.fori_loop(0, count_ref[step], add_tile, 0)
        for row in range(blocks):
            for column in range(blocks):
                out_ref[row * 128 : row * 128 + 128, column * 128 : column * 128 + 128] = total_ref[
                    row, column
                ].astype(out_ref.dtype)


def dense_blocks(rows, columns, values, counts, table, blocks):
    steps = rows.shape[0]
    tile = table.shape[1]
    side = blocks * tile
    whole = pl.BlockSpec(memory_space=pltpu.VMEM)
    scalars = pl.BlockSpec(memory_space=pltpu.SMEM)
    return pl.pallas_call(
        build_kernel,
        out_shape=[jax.ShapeDtypeStruct((side, side), table.dtype)] * steps,
        in_specs=[scalars] * 4 + [whole],
        out_specs=[whole] * steps,
        scratch_shapes=[pltpu.VMEM((blocks, blocks, tile, tile), jnp.float32)],
        compiler_params=pltpu.CompilerParams(vmem_limit_bytes=48 << 20),
        cost_estimate=pl.CostEstimate(flops=20_000_000, bytes_accessed=24 << 20, transcendentals=0),
    )(rows, columns, values, counts, table)


def exchanged(blocks, axis):
    return lax.all_to_all(blocks, axis, 0, 0, tiled=True)


def copies_from_all(array, axis):
    length = lax.axis_size(axis)
    return exchanged(jnp.broadcast_to(array[None], (length, *array.shape)), axis)


def on_device(
    features,
    weight_self,
    weight_neighbor,
    bias_vector,
    tile_row,
    tile_column,
    tile_value,
    tile_count,
    tile_table,
    cotangent,
):
    groups = lax.axis_size("blk")
    replicas = lax.axis_size("rep")
    steps = groups // replicas
    replica = lax.axis_index("rep")
    rows, width = features.shape
    tile = tile_table.shape[1]
    share = rows // replicas
    half = rows // 2
    bf16, f32 = jnp.bfloat16, jnp.float32

    first = permuted(features[:half], lambda g, r: (g + steps * r + 1, r))
    second = permuted(features[half:], lambda g, r: (g + steps * (r ^ 2) + 1, r ^ 2))
    matrices = dense_blocks(
        tile_row[0], tile_column[0], tile_value[0], tile_count[0], tile_table, rows // tile
    )
    first, second, matrices = lax.optimization_barrier((first, second, matrices))
    panel_1 = jnp.concatenate([first, second], axis=0)
    panel_2 = permuted(panel_1, lambda g, r: (g + 1, r))
    panel_0 = permuted(panel_1, lambda g, r: (g - 1, r))
    panel_3 = permuted(panel_2, lambda g, r: (g + 1, r))

    partial = jnp.dot(matrices[1], panel_1, preferred_element_type=f32)
    partial += jnp.dot(matrices[2], panel_2, preferred_element_type=f32)
    partial += jnp.dot(matrices[0], panel_0, preferred_element_type=f32)
    partial += jnp.dot(matrices[3], panel_3, preferred_element_type=f32)

    arrived = exchanged(partial.astype(bf16).reshape(replicas, share, width), "rep")
    own_aggregate = arrived.astype(f32).sum(axis=0).astype(bf16)
    aggregate = copies_from_all(own_aggregate, "rep").reshape(rows, width)

    pre = jnp.dot(features, weight_self, preferred_element_type=f32)
    pre = pre + jnp.dot(aggregate, weight_neighbor, preferred_element_type=f32) + bias_vector
    sigmoid_pre = jax.nn.sigmoid(pre)
    activations = (pre * sigmoid_pre).astype(bf16)
    derivative = sigmoid_pre * (1.0 + pre * (1.0 - sigmoid_pre))
    grad_pre = (cotangent.astype(f32) * derivative).astype(bf16)
    sent_back = lax.dot_general(
        grad_pre, weight_neighbor, CONTRACT_COLUMNS, preferred_element_type=f32
    ).astype(bf16)

    def pushed(step):
        return lax.dot_general(
            matrices[step], sent_back, CONTRACT_ROWS, preferred_element_type=f32
        )

    def to_left(array):
        return permuted(array, lambda g, r: (g - 1, r)).astype(f32)

    sum_3 = to_left(pushed(3).astype(bf16))
    sum_0 = permuted(pushed(0).astype(bf16), lambda g, r: (g + 1, r)).astype(f32)
    sum_2 = to_left((pushed(2) + sum_3).astype(bf16))
    sum_1 = (pushed(1) + sum_0 + sum_2).astype(bf16)
    first = permuted(sum_1[:half], lambda g, r: (g - steps * r - 1, r))
    second = permuted(sum_1[half:], lambda g, r: (g - steps * r - 1, r ^ 2))
    back = jnp.concatenate([first, second], axis=0)

    part = width // replicas
    own_features = lax.dynamic_slice_in_dim(features, replica * part, part, 1)
    own_inputs = lax.dynamic_slice_in_dim(aggregate, replica * part, part, 1)
    grad_both = lax.dot_general(
        jnp.concatenate([own_features, own_inputs], axis=1),
        grad_pre,
        CONTRACT_ROWS,
        preferred_element_type=f32,
    )
    grad_offset = jnp.sum(grad_pre.astype(f32), axis=0)
    packed = jnp.concatenate(
        [grad_both, grad_offset[None], jnp.zeros((15, width), f32)], axis=0
    )
    totals = exchanged(packed.reshape(groups, -1, 128), "blk").sum(axis=0)
    column_totals = copies_from_all(totals, "blk").reshape(2 * part + 16, width)

    own_grad = lax.dynamic_slice_in_dim(grad_pre, replica * share, share, 0)
    self_term = lax.dot_general(
        own_grad, weight_self, CONTRACT_COLUMNS, preferred_element_type=f32
    )
    arrived = exchanged(back.reshape(replicas, share, width), "rep")
    own_rows = (self_term + arrived.astype(f32).sum(axis=0)).astype(bf16)
    grad_features = copies_from_all(own_rows, "rep").reshape(rows, width)
    weights = copies_from_all(column_totals[: 2 * part], "rep")
    grad_self = weights[:, :part].reshape(width, width)
    grad_neighbor = weights[:, part:].reshape(width, width)
    grad_bias = column_totals[2 * part]
    return (activations, grad_features, grad_self, grad_neighbor, grad_bias)


def solution(mesh):
    placed = (
        P("blk", None),
        P(),
        P(),
        P(),
        P("blk", "rep", None),
        P("blk", "rep", None),
        P("blk", "rep", None),
        P("blk", "rep"),
        P(("blk", "rep"), None, None),
        P("blk", None),
    )
    return jax.shard_map(
        on_device,
        mesh=mesh,
        in_specs=placed,
        out_specs=(P("blk", None), P("blk", None), P(), P(), P()),
        check_vma=False,
    )
```

```python
import functools

import jax
import jax.numpy as jnp
from jax import lax
from jax.experimental import pallas as pl
from jax.experimental.pallas import tpu as pltpu
from jax.sharding import PartitionSpec as P

BOTH = ("blk", "rep")
CONTRACT_ROWS = (((0,), (0,)), ((), ()))
CONTRACT_COLUMNS = (((1,), (1,)), ((), ()))


def permuted(array, target):
    groups, replicas = lax.axis_size("blk"), lax.axis_size("rep")
    pairs = []
    for g in range(groups):
        for r in range(replicas):
            to_g, to_r = target(g, r)
            pairs.append((g * replicas + r, to_g % groups * replicas + to_r % replicas))
    return lax.ppermute(array, BOTH, pairs)


def build_kernel(row_ref, column_ref, value_ref, count_ref, table_ref, *refs):
    out_refs, total_ref = refs[:-1], refs[-1]
    blocks = total_ref.shape[0]
    for step, out_ref in enumerate(out_refs):
        total_ref[...] = jnp.zeros_like(total_ref)

        def add_tile(slot, unused, step=step):
            row = row_ref[step, slot]
            column = column_ref[step, slot]
            value = value_ref[step, slot]
            total_ref[row, column] += table_ref[value].astype(jnp.float32)
            return unused

        lax.fori_loop(0, count_ref[step], add_tile, 0)
        for row in range(blocks):
            for column in range(blocks):
                out_ref[row * 128 : row * 128 + 128, column * 128 : column * 128 + 128] = total_ref[
                    row, column
                ].astype(out_ref.dtype)


def dense_blocks(rows, columns, values, counts, table, blocks):
    steps = rows.shape[0]
    tile = table.shape[1]
    side = blocks * tile
    whole = pl.BlockSpec(memory_space=pltpu.VMEM)
    scalars = pl.BlockSpec(memory_space=pltpu.SMEM)
    return pl.pallas_call(
        build_kernel,
        out_shape=[jax.ShapeDtypeStruct((side, side), table.dtype)] * steps,
        in_specs=[scalars] * 4 + [whole],
        out_specs=[whole] * steps,
        scratch_shapes=[pltpu.VMEM((blocks, blocks, tile, tile), jnp.float32)],
        compiler_params=pltpu.CompilerParams(vmem_limit_bytes=48 << 20),
        cost_estimate=pl.CostEstimate(flops=20_000_000, bytes_accessed=24 << 20, transcendentals=0),
    )(rows, columns, values, counts, table)


def exchanged(blocks, axis):
    return lax.all_to_all(blocks, axis, 0, 0, tiled=True)


def copies_from_all(array, axis):
    length = lax.axis_size(axis)
    return exchanged(jnp.broadcast_to(array[None], (length, *array.shape)), axis)


def added(arrays):
    total = arrays[0].astype(jnp.float32)
    for array in arrays[1:]:
        total = total + array.astype(jnp.float32)
    return total


def on_device(
    features,
    weight_self,
    weight_neighbor,
    bias_vector,
    tile_row,
    tile_column,
    tile_value,
    tile_count,
    tile_table,
    cotangent,
):
    groups = lax.axis_size("blk")
    replicas = lax.axis_size("rep")
    steps = groups // replicas
    replica = lax.axis_index("rep")
    rows, width = features.shape
    tile = tile_table.shape[1]
    share = rows // replicas
    half = rows // 2
    bf16, f32 = jnp.bfloat16, jnp.float32

    first = permuted(features[:half], lambda g, r: (g + steps * r + 1, r))
    second = permuted(features[half:], lambda g, r: (g + steps * (r ^ 2) + 1, r ^ 2))
    matrices = dense_blocks(
        tile_row[0], tile_column[0], tile_value[0], tile_count[0], tile_table, rows // tile
    )
    first, second, matrices = lax.optimization_barrier((first, second, matrices))
    panel_1 = jnp.concatenate([first, second], axis=0)
    panel_2 = permuted(panel_1, lambda g, r: (g + 1, r))
    panel_0 = permuted(panel_1, lambda g, r: (g - 1, r))
    third = permuted(first, lambda g, r: (g + 2, r))
    fourth = permuted(second, lambda g, r: (g - 2, r - 1))
    panel_3 = jnp.concatenate([third, fourth], axis=0)

    partial = jnp.dot(matrices[1], panel_1, preferred_element_type=f32)
    partial += jnp.dot(matrices[2], panel_2, preferred_element_type=f32)
    partial += jnp.dot(matrices[0], panel_0, preferred_element_type=f32)
    partial += jnp.dot(matrices[3], panel_3, preferred_element_type=f32)

    arrived = exchanged(partial.astype(bf16).reshape(replicas, share, width), "rep")
    own_aggregate = added([arrived[i] for i in range(replicas)]).astype(bf16)
    aggregate = copies_from_all(own_aggregate, "rep").reshape(rows, width)

    pre = jnp.dot(features, weight_self, preferred_element_type=f32)
    pre = pre + jnp.dot(aggregate, weight_neighbor, preferred_element_type=f32) + bias_vector
    sigmoid_pre = jax.nn.sigmoid(pre)
    activations = (pre * sigmoid_pre).astype(bf16)
    derivative = sigmoid_pre * (1.0 + pre * (1.0 - sigmoid_pre))
    grad_pre = (cotangent.astype(f32) * derivative).astype(bf16)
    sent_back = lax.dot_general(
        grad_pre, weight_neighbor, CONTRACT_COLUMNS, preferred_element_type=f32
    ).astype(bf16)

    def pushed(step):
        return lax.dot_general(
            matrices[step], sent_back, CONTRACT_ROWS, preferred_element_type=f32
        )

    push_3 = pushed(3).astype(bf16)
    third = permuted(push_3[:half], lambda g, r: (g - 2, r))
    fourth = permuted(push_3[half:], lambda g, r: (g + 2, r + 1))
    sum_2 = permuted(pushed(2).astype(bf16), lambda g, r: (g - 1, r))
    sum_0 = permuted(pushed(0).astype(bf16), lambda g, r: (g + 1, r))

    part = width // replicas
    grad_self = lax.dot_general(features, grad_pre, CONTRACT_ROWS, preferred_element_type=f32)
    grad_neighbor = lax.dot_general(aggregate, grad_pre, CONTRACT_ROWS, preferred_element_type=f32)
    grad_offset = jnp.sum(grad_pre.astype(f32), axis=0)
    totals = jnp.concatenate(
        [
            lax.dynamic_slice_in_dim(grad_self, replica * part, part, 0),
            lax.dynamic_slice_in_dim(grad_neighbor, replica * part, part, 0),
            jnp.pad(grad_offset[None], ((0, 7), (0, 0))),
        ],
        axis=0,
    )
    def summed_over_bits(total, bits):
        for bit in bits:
            total = total + permuted(total, lambda g, r: (g ^ bit, r))
        return total

    bits = [1 << n for n in range(groups.bit_length() - 1)]
    totals = summed_over_bits(totals, bits[:2])

    sum_3 = jnp.concatenate([third, fourth], axis=0)
    sum_1 = pushed(1) + added([sum_0, sum_2, sum_3])
    blocks = sum_1.astype(bf16).reshape(replicas, share, width)
    blocks, totals = lax.optimization_barrier((blocks, totals))
    totals = summed_over_bits(totals, bits[2:])
    terms = []
    for offset in range(replicas):
        block = lax.dynamic_index_in_dim(blocks, (replica + offset) % replicas, 0, False)
        terms.append(
            permuted(block, lambda g, r, offset=offset: (g - steps * r - 1, r + offset))
        )

    own_grad = lax.dynamic_slice_in_dim(grad_pre, replica * share, share, 0)
    self_term = lax.dot_general(
        own_grad, weight_self, CONTRACT_COLUMNS, preferred_element_type=f32
    )
    own_rows = (self_term + added(terms)).astype(bf16)
    everything = copies_from_all(
        jnp.concatenate([own_rows, totals[: 2 * part].astype(bf16)], axis=0), "rep"
    )
    grad_features = everything[:, :share].reshape(rows, width)
    grad_self = everything[:, share : share + part].reshape(width, width).astype(f32)
    grad_neighbor = everything[:, share + part :].reshape(width, width).astype(f32)
    grad_bias = totals[2 * part]
    return (activations, grad_features, grad_self, grad_neighbor, grad_bias)


def solution(mesh):
    placed = (
        P("blk", None),
        P(),
        P(),
        P(),
        P("blk", "rep", None),
        P("blk", "rep", None),
        P("blk", "rep", None),
        P("blk", "rep"),
        P(("blk", "rep"), None, None),
        P("blk", None),
    )
    return jax.shard_map(
        on_device,
        mesh=mesh,
        in_specs=placed,
        out_specs=(P("blk", None), P("blk", None), P(), P(), P()),
        check_vma=False,
    )
```

```python
import functools

import jax
import jax.numpy as jnp
from jax import lax
from jax.experimental import pallas as pl
from jax.experimental.pallas import tpu as pltpu
from jax.sharding import PartitionSpec as P

BOTH = ("blk", "rep")
CONTRACT_ROWS = (((0,), (0,)), ((), ()))
CONTRACT_COLUMNS = (((1,), (1,)), ((), ()))


def permuted(array, target):
    groups, replicas = lax.axis_size("blk"), lax.axis_size("rep")
    pairs = []
    for g in range(groups):
        for r in range(replicas):
            to_g, to_r = target(g, r)
            pairs.append((g * replicas + r, to_g % groups * replicas + to_r % replicas))
    return lax.ppermute(array, BOTH, pairs)


def build_kernel(row_ref, column_ref, value_ref, count_ref, table_ref, *refs):
    out_refs, total_ref = refs[:-1], refs[-1]
    blocks = total_ref.shape[0]
    for step, out_ref in enumerate(out_refs):
        total_ref[...] = jnp.zeros_like(total_ref)

        def add_tile(slot, unused, step=step):
            row = row_ref[step, slot]
            column = column_ref[step, slot]
            value = value_ref[step, slot]
            total_ref[row, column] += table_ref[value].astype(jnp.float32)
            return unused

        lax.fori_loop(0, count_ref[step], add_tile, 0)
        for row in range(blocks):
            for column in range(blocks):
                out_ref[row * 128 : row * 128 + 128, column * 128 : column * 128 + 128] = total_ref[
                    row, column
                ].astype(out_ref.dtype)


def dense_blocks(rows, columns, values, counts, table, blocks):
    steps = rows.shape[0]
    tile = table.shape[1]
    side = blocks * tile
    whole = pl.BlockSpec(memory_space=pltpu.VMEM)
    scalars = pl.BlockSpec(memory_space=pltpu.SMEM)
    return pl.pallas_call(
        build_kernel,
        out_shape=[jax.ShapeDtypeStruct((side, side), table.dtype)] * steps,
        in_specs=[scalars] * 4 + [whole],
        out_specs=[whole] * steps,
        scratch_shapes=[pltpu.VMEM((blocks, blocks, tile, tile), jnp.float32)],
        compiler_params=pltpu.CompilerParams(vmem_limit_bytes=24 << 20),
        cost_estimate=pl.CostEstimate(flops=20_000_000, bytes_accessed=24 << 20, transcendentals=0),
    )(rows, columns, values, counts, table)


def exchanged(blocks, axis):
    return lax.all_to_all(blocks, axis, 0, 0, tiled=True)


def copies_from_all(array, axis):
    length = lax.axis_size(axis)
    return exchanged(jnp.broadcast_to(array[None], (length, *array.shape)), axis)


def added(arrays):
    total = arrays[0].astype(jnp.float32)
    for array in arrays[1:]:
        total = total + array.astype(jnp.float32)
    return total


def on_device(
    features,
    weight_self,
    weight_neighbor,
    bias_vector,
    tile_row,
    tile_column,
    tile_value,
    tile_count,
    tile_table,
    cotangent,
):
    groups = lax.axis_size("blk")
    replicas = lax.axis_size("rep")
    steps = groups // replicas
    replica = lax.axis_index("rep")
    rows, width = features.shape
    tile = tile_table.shape[1]
    share = rows // replicas
    half = rows // 2
    bf16, f32 = jnp.bfloat16, jnp.float32

    first = permuted(features[:half], lambda g, r: (g + steps * r + 1, r))
    second = permuted(features[half:], lambda g, r: (g + steps * (r ^ 2) + 1, r ^ 2))
    matrices = dense_blocks(
        tile_row[0], tile_column[0], tile_value[0], tile_count[0], tile_table, rows // tile
    )
    first, second, matrices = lax.optimization_barrier((first, second, matrices))
    panel_1 = jnp.concatenate([first, second], axis=0)
    panel_2 = permuted(panel_1, lambda g, r: (g + 1, r))
    panel_0 = permuted(panel_1, lambda g, r: (g - 1, r))
    third = permuted(first, lambda g, r: (g + 2, r))
    fourth = permuted(second, lambda g, r: (g - 2, r - 1))
    panel_3 = jnp.concatenate([third, fourth], axis=0)

    partial = jnp.dot(matrices[1], panel_1, preferred_element_type=f32)
    partial += jnp.dot(matrices[2], panel_2, preferred_element_type=f32)
    partial += jnp.dot(matrices[0], panel_0, preferred_element_type=f32)
    partial += jnp.dot(matrices[3], panel_3, preferred_element_type=f32)

    arrived = exchanged(partial.astype(bf16).reshape(replicas, share, width), "rep")
    own_aggregate = added([arrived[i] for i in range(replicas)]).astype(bf16)
    aggregate = copies_from_all(own_aggregate, "rep").reshape(rows, width)

    pre = jnp.dot(features, weight_self, preferred_element_type=f32)
    pre = pre + jnp.dot(aggregate, weight_neighbor, preferred_element_type=f32) + bias_vector
    sigmoid_pre = jax.nn.sigmoid(pre)
    activations = (pre * sigmoid_pre).astype(bf16)
    derivative = sigmoid_pre * (1.0 + pre * (1.0 - sigmoid_pre))
    grad_pre = (cotangent.astype(f32) * derivative).astype(bf16)
    sent_back = lax.dot_general(
        grad_pre, weight_neighbor, CONTRACT_COLUMNS, preferred_element_type=f32
    ).astype(bf16)

    def pushed(step):
        return lax.dot_general(
            matrices[step], sent_back, CONTRACT_ROWS, preferred_element_type=f32
        )

    push_3 = pushed(3).astype(bf16)
    push_2 = pushed(2).astype(bf16)
    push_0 = pushed(0).astype(bf16)
    third = permuted(push_3[:half], lambda g, r: (g - 2, r))
    fourth = permuted(push_3[half:], lambda g, r: (g + 2, r + 1))
    sum_2 = permuted(push_2, lambda g, r: (g - 1, r))
    sum_0 = permuted(push_0, lambda g, r: (g + 1, r))
    grad_pre, push_0 = lax.optimization_barrier((grad_pre, push_0))

    part = width // replicas
    grad_self = lax.dot_general(features, grad_pre, CONTRACT_ROWS, preferred_element_type=f32)
    grad_neighbor = lax.dot_general(aggregate, grad_pre, CONTRACT_ROWS, preferred_element_type=f32)
    grad_offset = jnp.sum(grad_pre.astype(f32), axis=0)
    totals = jnp.concatenate(
        [
            lax.dynamic_slice_in_dim(grad_self, replica * part, part, 0),
            lax.dynamic_slice_in_dim(grad_neighbor, replica * part, part, 0),
            jnp.pad(grad_offset[None], ((0, 7), (0, 0))),
        ],
        axis=0,
    )
    def summed_over_bits(total, bits):
        for bit in bits:
            total = total + permuted(total, lambda g, r: (g ^ bit, r))
        return total

    bits = [1 << n for n in range(groups.bit_length() - 1)]
    totals = summed_over_bits(totals, bits[:2])

    sum_3 = jnp.concatenate([third, fourth], axis=0)
    sum_1 = pushed(1) + added([sum_0, sum_2, sum_3])
    sum_1 = sum_1.astype(bf16)
    first, second, totals = lax.optimization_barrier((sum_1[:half], sum_1[half:], totals))
    first = permuted(first, lambda g, r: (g - steps * r - 1, r))
    second = permuted(second, lambda g, r: (g - steps * r - 1, r ^ 2))
    totals = summed_over_bits(totals, bits[2:])
    back = jnp.concatenate([first, second], axis=0).reshape(replicas, share, width)
    back, totals = lax.optimization_barrier((back, totals))
    arrived = exchanged(back, "rep")

    own_grad = lax.dynamic_slice_in_dim(grad_pre, replica * share, share, 0)
    self_term = lax.dot_general(
        own_grad, weight_self, CONTRACT_COLUMNS, preferred_element_type=f32
    )
    own_rows = (self_term + added([arrived[i] for i in range(replicas)])).astype(bf16)
    everything = copies_from_all(
        jnp.concatenate([own_rows, totals[: 2 * part].astype(bf16)], axis=0), "rep"
    )
    grad_features = everything[:, :share].reshape(rows, width)
    grad_self = everything[:, share : share + part].reshape(width, width).astype(f32)
    grad_neighbor = everything[:, share + part :].reshape(width, width).astype(f32)
    grad_bias = totals[2 * part]
    return (activations, grad_features, grad_self, grad_neighbor, grad_bias)


def solution(mesh):
    placed = (
        P("blk", None),
        P(),
        P(),
        P(),
        P("blk", "rep", None),
        P("blk", "rep", None),
        P("blk", "rep", None),
        P("blk", "rep"),
        P(("blk", "rep"), None, None),
        P("blk", None),
    )
    return jax.shard_map(
        on_device,
        mesh=mesh,
        in_specs=placed,
        out_specs=(P("blk", None), P("blk", None), P(), P(), P()),
        check_vma=False,
    )
```

```python
import functools

import jax
import jax.numpy as jnp
from jax import lax
from jax.experimental import pallas as pl
from jax.experimental.pallas import tpu as pltpu
from jax.sharding import PartitionSpec as P

BOTH = ("blk", "rep")
CONTRACT_ROWS = (((0,), (0,)), ((), ()))
CONTRACT_COLUMNS = (((1,), (1,)), ((), ()))


def permuted(array, target):
    groups, replicas = lax.axis_size("blk"), lax.axis_size("rep")
    pairs = []
    for g in range(groups):
        for r in range(replicas):
            to_g, to_r = target(g, r)
            pairs.append((g * replicas + r, to_g % groups * replicas + to_r % replicas))
    return lax.ppermute(array, BOTH, pairs)


def build_kernel(row_ref, column_ref, value_ref, count_ref, table_ref, *refs):
    out_refs, total_ref = refs[:-1], refs[-1]
    blocks = total_ref.shape[0]
    for step, out_ref in enumerate(out_refs):
        total_ref[...] = jnp.zeros_like(total_ref)

        def add_tile(slot, unused, step=step):
            row = row_ref[step, slot]
            column = column_ref[step, slot]
            value = value_ref[step, slot]
            total_ref[row, column] += table_ref[value].astype(jnp.float32)
            return unused

        lax.fori_loop(0, count_ref[step], add_tile, 0)
        for row in range(blocks):
            for column in range(blocks):
                out_ref[row * 128 : row * 128 + 128, column * 128 : column * 128 + 128] = total_ref[
                    row, column
                ].astype(out_ref.dtype)


def dense_blocks(rows, columns, values, counts, table, blocks):
    steps = rows.shape[0]
    tile = table.shape[1]
    side = blocks * tile
    whole = pl.BlockSpec(memory_space=pltpu.VMEM)
    scalars = pl.BlockSpec(memory_space=pltpu.SMEM)
    return pl.pallas_call(
        build_kernel,
        out_shape=[jax.ShapeDtypeStruct((side, side), table.dtype)] * steps,
        in_specs=[scalars] * 4 + [whole],
        out_specs=[whole] * steps,
        scratch_shapes=[pltpu.VMEM((blocks, blocks, tile, tile), jnp.float32)],
        compiler_params=pltpu.CompilerParams(vmem_limit_bytes=24 << 20),
        cost_estimate=pl.CostEstimate(flops=20_000_000, bytes_accessed=24 << 20, transcendentals=0),
    )(rows, columns, values, counts, table)


def exchanged(blocks, axis):
    return lax.all_to_all(blocks, axis, 0, 0, tiled=True)


def copies_from_all(array, axis):
    length = lax.axis_size(axis)
    return exchanged(jnp.broadcast_to(array[None], (length, *array.shape)), axis)


def added(arrays):
    total = arrays[0].astype(jnp.float32)
    for array in arrays[1:]:
        total = total + array.astype(jnp.float32)
    return total


def on_device(
    features,
    weight_self,
    weight_neighbor,
    bias_vector,
    tile_row,
    tile_column,
    tile_value,
    tile_count,
    tile_table,
    cotangent,
):
    groups = lax.axis_size("blk")
    replicas = lax.axis_size("rep")
    steps = groups // replicas
    replica = lax.axis_index("rep")
    rows, width = features.shape
    tile = tile_table.shape[1]
    share = rows // replicas
    half = rows // 2
    bf16, f32 = jnp.bfloat16, jnp.float32

    first = permuted(features[:half], lambda g, r: (g + steps * r + 1, r))
    second = permuted(features[half:], lambda g, r: (g + steps * (r ^ 2) + 1, r ^ 2))
    matrices = dense_blocks(
        tile_row[0], tile_column[0], tile_value[0], tile_count[0], tile_table, rows // tile
    )
    first, second, matrices = lax.optimization_barrier((first, second, matrices))
    panel_1 = jnp.concatenate([first, second], axis=0)
    panel_2 = permuted(panel_1, lambda g, r: (g + 1, r))
    panel_0 = permuted(panel_1, lambda g, r: (g - 1, r))
    panel_3 = permuted(panel_2, lambda g, r: (g + 1, r))

    partial = jnp.dot(matrices[1], panel_1, preferred_element_type=f32)
    partial += jnp.dot(matrices[2], panel_2, preferred_element_type=f32)
    partial += jnp.dot(matrices[0], panel_0, preferred_element_type=f32)
    partial += jnp.dot(matrices[3], panel_3, preferred_element_type=f32)

    arrived = exchanged(partial.astype(bf16).reshape(replicas, share, width), "rep")
    own_aggregate = added([arrived[i] for i in range(replicas)]).astype(bf16)
    aggregate = copies_from_all(own_aggregate, "rep").reshape(rows, width)

    pre = jnp.dot(features, weight_self, preferred_element_type=f32)
    pre = pre + jnp.dot(aggregate, weight_neighbor, preferred_element_type=f32) + bias_vector
    sigmoid_pre = jax.nn.sigmoid(pre)
    activations = (pre * sigmoid_pre).astype(bf16)
    derivative = sigmoid_pre * (1.0 + pre * (1.0 - sigmoid_pre))
    grad_pre = (cotangent.astype(f32) * derivative).astype(bf16)
    sent_back = lax.dot_general(
        grad_pre, weight_neighbor, CONTRACT_COLUMNS, preferred_element_type=f32
    ).astype(bf16)

    def pushed(step):
        return lax.dot_general(
            matrices[step], sent_back, CONTRACT_ROWS, preferred_element_type=f32
        )

    part = width // replicas
    is_even = lax.axis_index("blk") % 2 == 0
    grad_self = lax.dot_general(features, grad_pre, CONTRACT_ROWS, preferred_element_type=f32)
    grad_neighbor = lax.dot_general(aggregate, grad_pre, CONTRACT_ROWS, preferred_element_type=f32)
    grad_offset = jnp.sum(grad_pre.astype(f32), axis=0)
    offset_rows = jnp.broadcast_to(
        jnp.pad(grad_offset[None], ((0, 7), (0, 0))), (replicas, 8, width)
    )

    def rider(chosen):
        return jnp.concatenate([chosen.reshape(replicas, part, width), offset_rows], axis=1)

    rider_even = rider(jnp.where(is_even, grad_self, grad_neighbor))
    rider_odd = rider(jnp.where(is_even, grad_neighbor, grad_self))

    def with_rider(step, received):
        main = pushed(step).reshape(replicas, share, width)
        extra = rider_odd if step % 2 else rider_even
        for array in received:
            main = main + array[:, :share].astype(f32)
            extra = extra + array[:, share:].astype(f32)
        return jnp.concatenate([main.astype(bf16), extra.astype(bf16)], axis=1)

    sum_3 = permuted(with_rider(3, []), lambda g, r: (g - 1, r))
    sum_0 = permuted(with_rider(0, []), lambda g, r: (g + 1, r))
    sum_2 = permuted(with_rider(2, [sum_3]), lambda g, r: (g - 1, r))
    sum_1 = with_rider(1, [sum_0, sum_2])
    first = permuted(sum_1[: replicas // 2], lambda g, r: (g - steps * r - 1, r))
    second = permuted(sum_1[replicas // 2 :], lambda g, r: (g - steps * r - 1, r ^ 2))
    arrived = exchanged(jnp.concatenate([first, second], axis=0), "rep")

    own_grad = lax.dynamic_slice_in_dim(grad_pre, replica * share, share, 0)
    self_term = lax.dot_general(
        own_grad, weight_self, CONTRACT_COLUMNS, preferred_element_type=f32
    )
    own_extra = added([arrived[i, share:] for i in range(replicas)])
    own_part = own_extra[:part].astype(bf16)
    other_part = permuted(own_part, lambda g, r: (g ^ 1, r))
    own_rows = (self_term + added([arrived[i, :share] for i in range(replicas)])).astype(bf16)
    everything = copies_from_all(
        jnp.concatenate(
            [
                own_rows,
                jnp.where(is_even, own_part, other_part),
                jnp.where(is_even, other_part, own_part),
            ],
            axis=0,
        ),
        "rep",
    )
    grad_features = everything[:, :share].reshape(rows, width)
    grad_self = everything[:, share : share + part].reshape(width, width).astype(f32)
    grad_neighbor = everything[:, share + part :].reshape(width, width).astype(f32)
    grad_bias = own_extra[part]
    return (activations, grad_features, grad_self, grad_neighbor, grad_bias)


def solution(mesh):
    placed = (
        P("blk", None),
        P(),
        P(),
        P(),
        P("blk", "rep", None),
        P("blk", "rep", None),
        P("blk", "rep", None),
        P("blk", "rep"),
        P(("blk", "rep"), None, None),
        P("blk", None),
    )
    return jax.shard_map(
        on_device,
        mesh=mesh,
        in_specs=placed,
        out_specs=(P("blk", None), P("blk", None), P(), P(), P()),
        check_vma=False,
    )
```

```python
import functools

import jax
import jax.numpy as jnp
from jax import lax
from jax.experimental import pallas as pl
from jax.experimental.pallas import tpu as pltpu
from jax.sharding import PartitionSpec as P

BOTH = ("blk", "rep")
CONTRACT_ROWS = (((0,), (0,)), ((), ()))
CONTRACT_COLUMNS = (((1,), (1,)), ((), ()))


def permuted(array, target):
    groups, replicas = lax.axis_size("blk"), lax.axis_size("rep")
    pairs = []
    for g in range(groups):
        for r in range(replicas):
            to_g, to_r = target(g, r)
            pairs.append((g * replicas + r, to_g % groups * replicas + to_r % replicas))
    return lax.ppermute(array, BOTH, pairs)


def build_kernel(row_ref, column_ref, value_ref, count_ref, table_ref, *refs):
    out_refs, total_ref = refs[:-1], refs[-1]
    blocks = total_ref.shape[0]
    for step, out_ref in enumerate(out_refs):
        total_ref[...] = jnp.zeros_like(total_ref)

        def add_tile(slot, unused, step=step):
            row = row_ref[step, slot]
            column = column_ref[step, slot]
            value = value_ref[step, slot]
            total_ref[row, column] += table_ref[value].astype(jnp.float32)
            return unused

        lax.fori_loop(0, count_ref[step], add_tile, 0)
        for row in range(blocks):
            for column in range(blocks):
                out_ref[row * 128 : row * 128 + 128, column * 128 : column * 128 + 128] = total_ref[
                    row, column
                ].astype(out_ref.dtype)


def dense_blocks(rows, columns, values, counts, table, blocks):
    steps = rows.shape[0]
    tile = table.shape[1]
    side = blocks * tile
    whole = pl.BlockSpec(memory_space=pltpu.VMEM)
    scalars = pl.BlockSpec(memory_space=pltpu.SMEM)
    return pl.pallas_call(
        build_kernel,
        out_shape=[jax.ShapeDtypeStruct((side, side), table.dtype)] * steps,
        in_specs=[scalars] * 4 + [whole],
        out_specs=[whole] * steps,
        scratch_shapes=[pltpu.VMEM((blocks, blocks, tile, tile), jnp.float32)],
        compiler_params=pltpu.CompilerParams(vmem_limit_bytes=24 << 20),
        cost_estimate=pl.CostEstimate(flops=20_000_000, bytes_accessed=24 << 20, transcendentals=0),
    )(rows, columns, values, counts, table)


def exchanged(blocks, axis):
    return lax.all_to_all(blocks, axis, 0, 0, tiled=True)


def copies_from_all(array, axis):
    length = lax.axis_size(axis)
    return exchanged(jnp.broadcast_to(array[None], (length, *array.shape)), axis)


def added(arrays):
    total = arrays[0].astype(jnp.float32)
    for array in arrays[1:]:
        total = total + array.astype(jnp.float32)
    return total


def on_device(
    features,
    weight_self,
    weight_neighbor,
    bias_vector,
    tile_row,
    tile_column,
    tile_value,
    tile_count,
    tile_table,
    cotangent,
):
    groups = lax.axis_size("blk")
    replicas = lax.axis_size("rep")
    steps = groups // replicas
    replica = lax.axis_index("rep")
    rows, width = features.shape
    tile = tile_table.shape[1]
    share = rows // replicas
    half = rows // 2
    bf16, f32 = jnp.bfloat16, jnp.float32

    first = permuted(features[:half], lambda g, r: (g + steps * r + 1, r))
    second = permuted(features[half:], lambda g, r: (g + steps * (r ^ 2) + 1, r ^ 2))
    matrices = dense_blocks(
        tile_row[0], tile_column[0], tile_value[0], tile_count[0], tile_table, rows // tile
    )
    first, second, matrices = lax.optimization_barrier((first, second, matrices))
    panel_1 = jnp.concatenate([first, second], axis=0)
    panel_2 = permuted(panel_1, lambda g, r: (g + 1, r))
    panel_0 = permuted(panel_1, lambda g, r: (g - 1, r))
    panel_3 = permuted(panel_2, lambda g, r: (g + 1, r))

    partial = jnp.dot(matrices[1], panel_1, preferred_element_type=f32)
    partial += jnp.dot(matrices[2], panel_2, preferred_element_type=f32)
    partial += jnp.dot(matrices[0], panel_0, preferred_element_type=f32)
    partial += jnp.dot(matrices[3], panel_3, preferred_element_type=f32)

    arrived = exchanged(partial.astype(bf16).reshape(replicas, share, width), "rep")
    own_aggregate = added([arrived[i] for i in range(replicas)]).astype(bf16)
    aggregate = copies_from_all(own_aggregate, "rep").reshape(rows, width)

    pre = jnp.dot(features, weight_self, preferred_element_type=f32)
    pre = pre + jnp.dot(aggregate, weight_neighbor, preferred_element_type=f32) + bias_vector
    sigmoid_pre = jax.nn.sigmoid(pre)
    activations = (pre * sigmoid_pre).astype(bf16)
    derivative = sigmoid_pre * (1.0 + pre * (1.0 - sigmoid_pre))
    grad_pre = (cotangent.astype(f32) * derivative).astype(bf16)
    sent_back = lax.dot_general(
        grad_pre, weight_neighbor, CONTRACT_COLUMNS, preferred_element_type=f32
    ).astype(bf16)

    def pushed(step):
        return lax.dot_general(
            matrices[step], sent_back, CONTRACT_ROWS, preferred_element_type=f32
        )

    part = 2 * width // steps // replicas
    group = lax.axis_index("blk")
    grad_self = lax.dot_general(features, grad_pre, CONTRACT_ROWS, preferred_element_type=f32)
    grad_neighbor = lax.dot_general(aggregate, grad_pre, CONTRACT_ROWS, preferred_element_type=f32)
    quarters = jnp.concatenate([grad_self, grad_neighbor], axis=0).reshape(
        steps, replicas, part, width
    )
    grad_offset = jnp.sum(grad_pre.astype(f32), axis=0)
    offset_rows = jnp.broadcast_to(
        jnp.pad(grad_offset[None], ((0, 7), (0, 0))), (replicas, 8, width)
    )

    def with_rider(step, received):
        main = pushed(step).reshape(replicas, share, width)
        quarter = lax.dynamic_index_in_dim(quarters, (group + steps - step) % steps, 0, False)
        extra = jnp.concatenate([quarter, offset_rows], axis=1)
        for array in received:
            main = main + array[:, :share].astype(f32)
            extra = extra + array[:, share:].astype(f32)
        return jnp.concatenate([main.astype(bf16), extra.astype(bf16)], axis=1)

    sum_3 = permuted(with_rider(3, []), lambda g, r: (g - 1, r))
    sum_0 = permuted(with_rider(0, []), lambda g, r: (g + 1, r))
    sum_2 = permuted(with_rider(2, [sum_3]), lambda g, r: (g - 1, r))
    sum_1 = with_rider(1, [sum_0, sum_2])

    pairs = sum_1.reshape(replicas // 2, 2, -1, width)
    terms = []
    for bits in range(replicas // 2):
        block = lax.dynamic_index_in_dim(pairs, (replica // 2) ^ bits, 0, False)
        terms.append(
            permuted(block, lambda g, r, bits=bits: (g - steps * r - 1, r ^ (2 * bits)))
        )
    halves = added(terms)
    kept = lax.dynamic_index_in_dim(halves, replica % 2, 0, False)
    given = lax.dynamic_index_in_dim(halves, 1 - replica % 2, 0, False)
    total = kept + permuted(given.astype(bf16), lambda g, r: (g, r ^ 1)).astype(f32)

    own_grad = lax.dynamic_slice_in_dim(grad_pre, replica * share, share, 0)
    self_term = lax.dot_general(
        own_grad, weight_self, CONTRACT_COLUMNS, preferred_element_type=f32
    )
    own_part = total[share : share + part].astype(bf16)
    found = [own_part]
    for bits in range(1, steps):
        found.append(permuted(own_part, lambda g, r, bits=bits: (g ^ bits, r)))
    ordered = [lax.select_n((group % steps) ^ n, *found) for n in range(steps)]
    own_rows = (self_term + total[:share]).astype(bf16)
    everything = copies_from_all(jnp.concatenate([own_rows, *ordered], axis=0), "rep")
    grad_features = everything[:, :share].reshape(rows, width)
    weights = everything[:, share:].reshape(replicas, steps, part, width)
    weights = jnp.moveaxis(weights, 0, 1).astype(f32).reshape(2, width, width)
    grad_bias = total[share + part]
    return (activations, grad_features, weights[0], weights[1], grad_bias)


def solution(mesh):
    placed = (
        P("blk", None),
        P(),
        P(),
        P(),
        P("blk", "rep", None),
        P("blk", "rep", None),
        P("blk", "rep", None),
        P("blk", "rep"),
        P(("blk", "rep"), None, None),
        P("blk", None),
    )
    return jax.shard_map(
        on_device,
        mesh=mesh,
        in_specs=placed,
        out_specs=(P("blk", None), P("blk", None), P(), P(), P()),
        check_vma=False,
    )
```

```python
import functools

import jax
import jax.numpy as jnp
from jax import lax
from jax.experimental import pallas as pl
from jax.experimental.pallas import tpu as pltpu
from jax.sharding import PartitionSpec as P

BOTH = ("blk", "rep")
CONTRACT_ROWS = (((0,), (0,)), ((), ()))
CONTRACT_COLUMNS = (((1,), (1,)), ((), ()))


def permuted(array, target):
    groups, replicas = lax.axis_size("blk"), lax.axis_size("rep")
    pairs = []
    for g in range(groups):
        for r in range(replicas):
            to_g, to_r = target(g, r)
            pairs.append((g * replicas + r, to_g % groups * replicas + to_r % replicas))
    return lax.ppermute(array, BOTH, pairs)


def build_kernel(row_ref, column_ref, value_ref, count_ref, table_ref, *refs):
    out_refs, total_ref = refs[:-1], refs[-1]
    blocks = total_ref.shape[0]
    for step, out_ref in enumerate(out_refs):
        total_ref[...] = jnp.zeros_like(total_ref)

        def add_tile(slot, unused, step=step):
            row = row_ref[step, slot]
            column = column_ref[step, slot]
            value = value_ref[step, slot]
            total_ref[row, column] += table_ref[value].astype(jnp.float32)
            return unused

        lax.fori_loop(0, count_ref[step], add_tile, 0)
        for row in range(blocks):
            for column in range(blocks):
                out_ref[row * 128 : row * 128 + 128, column * 128 : column * 128 + 128] = total_ref[
                    row, column
                ].astype(out_ref.dtype)


def dense_blocks(rows, columns, values, counts, table, blocks):
    steps = rows.shape[0]
    tile = table.shape[1]
    side = blocks * tile
    whole = pl.BlockSpec(memory_space=pltpu.VMEM)
    scalars = pl.BlockSpec(memory_space=pltpu.SMEM)
    return pl.pallas_call(
        build_kernel,
        out_shape=[jax.ShapeDtypeStruct((side, side), table.dtype)] * steps,
        in_specs=[scalars] * 4 + [whole],
        out_specs=[whole] * steps,
        scratch_shapes=[pltpu.VMEM((blocks, blocks, tile, tile), jnp.float32)],
        compiler_params=pltpu.CompilerParams(vmem_limit_bytes=24 << 20),
        cost_estimate=pl.CostEstimate(flops=20_000_000, bytes_accessed=24 << 20, transcendentals=0),
    )(rows, columns, values, counts, table)


def exchanged(blocks, axis):
    return lax.all_to_all(blocks, axis, 0, 0, tiled=True)


def copies_from_all(array, axis):
    length = lax.axis_size(axis)
    return exchanged(jnp.broadcast_to(array[None], (length, *array.shape)), axis)


def added(arrays):
    total = arrays[0].astype(jnp.float32)
    for array in arrays[1:]:
        total = total + array.astype(jnp.float32)
    return total


def on_device(
    features,
    weight_self,
    weight_neighbor,
    bias_vector,
    tile_row,
    tile_column,
    tile_value,
    tile_count,
    tile_table,
    cotangent,
):
    groups = lax.axis_size("blk")
    replicas = lax.axis_size("rep")
    steps = groups // replicas
    replica = lax.axis_index("rep")
    rows, width = features.shape
    tile = tile_table.shape[1]
    share = rows // replicas
    half = rows // 2
    bf16, f32 = jnp.bfloat16, jnp.float32

    first = permuted(features[:half], lambda g, r: (g + steps * r + 1, r))
    second = permuted(features[half:], lambda g, r: (g + steps * (r ^ 2) + 1, r ^ 2))
    matrices = dense_blocks(
        tile_row[0], tile_column[0], tile_value[0], tile_count[0], tile_table, rows // tile
    )
    first, second, matrices = lax.optimization_barrier((first, second, matrices))
    panel_1 = jnp.concatenate([first, second], axis=0)
    panel_2 = permuted(panel_1, lambda g, r: (g + 1, r))
    panel_0 = permuted(panel_1, lambda g, r: (g - 1, r))
    panel_3 = permuted(panel_2, lambda g, r: (g + 1, r))

    partial = jnp.dot(matrices[1], panel_1, preferred_element_type=f32)
    partial += jnp.dot(matrices[2], panel_2, preferred_element_type=f32)
    partial += jnp.dot(matrices[0], panel_0, preferred_element_type=f32)
    partial += jnp.dot(matrices[3], panel_3, preferred_element_type=f32)

    arrived = exchanged(partial.astype(bf16).reshape(replicas, share, width), "rep")
    own_aggregate = added([arrived[i] for i in range(replicas)]).astype(bf16)
    aggregate = copies_from_all(own_aggregate, "rep").reshape(rows, width)

    pre = jnp.dot(features, weight_self, preferred_element_type=f32)
    pre = pre + jnp.dot(aggregate, weight_neighbor, preferred_element_type=f32) + bias_vector
    sigmoid_pre = jax.nn.sigmoid(pre)
    activations = (pre * sigmoid_pre).astype(bf16)
    derivative = sigmoid_pre * (1.0 + pre * (1.0 - sigmoid_pre))
    grad_pre = (cotangent.astype(f32) * derivative).astype(bf16)
    sent_back = lax.dot_general(
        grad_pre, weight_neighbor, CONTRACT_COLUMNS, preferred_element_type=f32
    ).astype(bf16)

    def pushed(step):
        return lax.dot_general(
            matrices[step], sent_back, CONTRACT_ROWS, preferred_element_type=f32
        )

    push_3 = pushed(3).astype(bf16)
    push_0 = pushed(0).astype(bf16)
    sum_3 = permuted(push_3, lambda g, r: (g - 1, r))
    sum_0 = permuted(push_0, lambda g, r: (g + 1, r))
    grad_pre, push_0, push_3 = lax.optimization_barrier((grad_pre, push_0, push_3))

    part = width // replicas
    grad_self = lax.dot_general(features, grad_pre, CONTRACT_ROWS, preferred_element_type=f32)
    grad_neighbor = lax.dot_general(aggregate, grad_pre, CONTRACT_ROWS, preferred_element_type=f32)
    grad_offset = jnp.sum(grad_pre.astype(f32), axis=0)
    totals = jnp.concatenate(
        [
            lax.dynamic_slice_in_dim(grad_self, replica * part, part, 0),
            lax.dynamic_slice_in_dim(grad_neighbor, replica * part, part, 0),
            jnp.pad(grad_offset[None], ((0, 7), (0, 0))),
        ],
        axis=0,
    )
    def summed_over_bits(total, bits):
        for bit in bits:
            total = total + permuted(total, lambda g, r: (g ^ bit, r))
        return total

    bits = [1 << n for n in range(groups.bit_length() - 1)]
    totals = summed_over_bits(totals, bits[:1])
    sum_3, totals = lax.optimization_barrier((sum_3, totals))
    sum_2 = permuted((pushed(2) + sum_3.astype(f32)).astype(bf16), lambda g, r: (g - 1, r))
    totals = summed_over_bits(totals, bits[-1:])
    sum_2, totals = lax.optimization_barrier((sum_2, totals))
    sum_1 = (pushed(1) + added([sum_0, sum_2])).astype(bf16)

    first = permuted(sum_1[:half], lambda g, r: (g - steps * r - 1, r))
    second = permuted(sum_1[half:], lambda g, r: (g, r ^ 2))
    second, totals = lax.optimization_barrier((second, totals))
    second = permuted(second, lambda g, r: (g - steps * (r ^ 2) - 1, r))
    totals = summed_over_bits(totals, bits[1:-2])
    last = permuted(totals, lambda g, r: (g ^ bits[-2], r))
    back = jnp.concatenate([first, second], axis=0).reshape(replicas, share, width)
    arrived = exchanged(back, "rep")
    last, arrived = lax.optimization_barrier((last, arrived))
    totals = totals + last

    own_grad = lax.dynamic_slice_in_dim(grad_pre, replica * share, share, 0)
    self_term = lax.dot_general(
        own_grad, weight_self, CONTRACT_COLUMNS, preferred_element_type=f32
    )
    own_rows = (self_term + added([arrived[i] for i in range(replicas)])).astype(bf16)
    everything = copies_from_all(
        jnp.concatenate([own_rows, totals[: 2 * part].astype(bf16)], axis=0), "rep"
    )
    grad_features = everything[:, :share].reshape(rows, width)
    grad_self = everything[:, share : share + part].reshape(width, width).astype(f32)
    grad_neighbor = everything[:, share + part :].reshape(width, width).astype(f32)
    grad_bias = totals[2 * part]
    return (activations, grad_features, grad_self, grad_neighbor, grad_bias)


def solution(mesh):
    placed = (
        P("blk", None),
        P(),
        P(),
        P(),
        P("blk", "rep", None),
        P("blk", "rep", None),
        P("blk", "rep", None),
        P("blk", "rep"),
        P(("blk", "rep"), None, None),
        P("blk", None),
    )
    return jax.shard_map(
        on_device,
        mesh=mesh,
        in_specs=placed,
        out_specs=(P("blk", None), P("blk", None), P(), P(), P()),
        check_vma=False,
    )
```

```python
import functools

import jax
import jax.numpy as jnp
from jax import lax
from jax.experimental import pallas as pl
from jax.experimental.pallas import tpu as pltpu
from jax.sharding import PartitionSpec as P

BOTH = ("blk", "rep")
CONTRACT_ROWS = (((0,), (0,)), ((), ()))
CONTRACT_COLUMNS = (((1,), (1,)), ((), ()))


def permuted(array, target):
    groups, replicas = lax.axis_size("blk"), lax.axis_size("rep")
    pairs = []
    for g in range(groups):
        for r in range(replicas):
            to_g, to_r = target(g, r)
            pairs.append((g * replicas + r, to_g % groups * replicas + to_r % replicas))
    return lax.ppermute(array, BOTH, pairs)


def build_kernel(row_ref, column_ref, value_ref, count_ref, table_ref, *refs):
    out_refs, total_ref = refs[:-1], refs[-1]
    blocks = total_ref.shape[0]
    for step, out_ref in enumerate(out_refs):
        total_ref[...] = jnp.zeros_like(total_ref)

        def add_tile(slot, unused, step=step):
            row = row_ref[step, slot]
            column = column_ref[step, slot]
            value = value_ref[step, slot]
            total_ref[row, column] += table_ref[value].astype(jnp.float32)
            return unused

        lax.fori_loop(0, count_ref[step], add_tile, 0)
        for row in range(blocks):
            for column in range(blocks):
                out_ref[row * 128 : row * 128 + 128, column * 128 : column * 128 + 128] = total_ref[
                    row, column
                ].astype(out_ref.dtype)


def dense_blocks(rows, columns, values, counts, table, blocks):
    steps = rows.shape[0]
    tile = table.shape[1]
    side = blocks * tile
    whole = pl.BlockSpec(memory_space=pltpu.VMEM)
    scalars = pl.BlockSpec(memory_space=pltpu.SMEM)
    return pl.pallas_call(
        build_kernel,
        out_shape=[jax.ShapeDtypeStruct((side, side), table.dtype)] * steps,
        in_specs=[scalars] * 4 + [whole],
        out_specs=[whole] * steps,
        scratch_shapes=[pltpu.VMEM((blocks, blocks, tile, tile), jnp.float32)],
        compiler_params=pltpu.CompilerParams(vmem_limit_bytes=24 << 20),
        cost_estimate=pl.CostEstimate(flops=20_000_000, bytes_accessed=24 << 20, transcendentals=0),
    )(rows, columns, values, counts, table)


def exchanged(blocks, axis):
    return lax.all_to_all(blocks, axis, 0, 0, tiled=True)


def copies_from_all(array, axis):
    length = lax.axis_size(axis)
    return exchanged(jnp.broadcast_to(array[None], (length, *array.shape)), axis)


def added(arrays):
    total = arrays[0].astype(jnp.float32)
    for array in arrays[1:]:
        total = total + array.astype(jnp.float32)
    return total


def on_device(
    features,
    weight_self,
    weight_neighbor,
    bias_vector,
    tile_row,
    tile_column,
    tile_value,
    tile_count,
    tile_table,
    cotangent,
):
    groups = lax.axis_size("blk")
    replicas = lax.axis_size("rep")
    steps = groups // replicas
    replica = lax.axis_index("rep")
    rows, width = features.shape
    tile = tile_table.shape[1]
    share = rows // replicas
    half = rows // 2
    bf16, f32 = jnp.bfloat16, jnp.float32

    first = permuted(features[:half], lambda g, r: (g + steps * r + 1, r))
    second = permuted(features[half:], lambda g, r: (g + steps * (r ^ 2) + 1, r ^ 2))
    matrices = dense_blocks(
        tile_row[0], tile_column[0], tile_value[0], tile_count[0], tile_table, rows // tile
    )
    first, second, matrices = lax.optimization_barrier((first, second, matrices))
    panel_1 = jnp.concatenate([first, second], axis=0)
    panel_2 = permuted(panel_1, lambda g, r: (g + 1, r))
    panel_0 = permuted(panel_1, lambda g, r: (g - 1, r))
    panel_3 = permuted(panel_2, lambda g, r: (g + 1, r))

    partial = jnp.dot(matrices[1], panel_1, preferred_element_type=f32)
    partial += jnp.dot(matrices[2], panel_2, preferred_element_type=f32)
    partial += jnp.dot(matrices[0], panel_0, preferred_element_type=f32)
    partial += jnp.dot(matrices[3], panel_3, preferred_element_type=f32)

    arrived = exchanged(partial.astype(bf16).reshape(replicas, share, width), "rep")
    own_aggregate = added([arrived[i] for i in range(replicas)]).astype(bf16)
    aggregate = copies_from_all(own_aggregate, "rep").reshape(rows, width)

    pre = jnp.dot(features, weight_self, preferred_element_type=f32)
    pre = pre + jnp.dot(aggregate, weight_neighbor, preferred_element_type=f32) + bias_vector
    sigmoid_pre = jax.nn.sigmoid(pre)
    activations = (pre * sigmoid_pre).astype(bf16)
    derivative = sigmoid_pre * (1.0 + pre * (1.0 - sigmoid_pre))
    grad_pre = (cotangent.astype(f32) * derivative).astype(bf16)
    sent_back = lax.dot_general(
        grad_pre, weight_neighbor, CONTRACT_COLUMNS, preferred_element_type=f32
    ).astype(bf16)

    def pushed(step):
        return lax.dot_general(
            matrices[step], sent_back, CONTRACT_ROWS, preferred_element_type=f32
        )

    push_3 = pushed(3).astype(bf16)
    push_0 = pushed(0).astype(bf16)
    sum_3 = permuted(push_3, lambda g, r: (g - 1, r))
    sum_0 = permuted(push_0, lambda g, r: (g + 1, r))
    grad_pre, push_0, push_3 = lax.optimization_barrier((grad_pre, push_0, push_3))

    part = width // replicas
    grad_self = lax.dot_general(features, grad_pre, CONTRACT_ROWS, preferred_element_type=f32)
    grad_neighbor = lax.dot_general(aggregate, grad_pre, CONTRACT_ROWS, preferred_element_type=f32)
    grad_offset = jnp.sum(grad_pre.astype(f32), axis=0)
    totals = jnp.concatenate(
        [
            lax.dynamic_slice_in_dim(grad_self, replica * part, part, 0),
            lax.dynamic_slice_in_dim(grad_neighbor, replica * part, part, 0),
            jnp.pad(grad_offset[None], ((0, 7), (0, 0))),
        ],
        axis=0,
    )
    def across(array, bit):
        return permuted(array, lambda g, r: (g ^ bit, r))

    core, near, middle, far, side = [1 << n for n in range(groups.bit_length() - 1)]
    totals = totals + across(totals, core)
    sum_3, sum_0, totals = lax.optimization_barrier((sum_3, sum_0, totals))
    sum_2 = permuted((pushed(2) + sum_3.astype(f32)).astype(bf16), lambda g, r: (g - 1, r))
    totals = totals + across(totals, side)
    sum_2, totals = lax.optimization_barrier((sum_2, totals))
    sum_1 = (pushed(1) + added([sum_0, sum_2])).astype(bf16)

    cut = rows * 5 // 8
    first = permuted(sum_1[:cut], lambda g, r: (g - steps * r - 1, r))
    second = permuted(sum_1[cut:], lambda g, r: (g, r ^ 2))
    met = across(totals, near)
    second, met = lax.optimization_barrier((second, met))
    totals = totals + met
    second = permuted(second, lambda g, r: (g - steps * (r ^ 2) - 1, r))
    met = across(totals, middle)
    first, met = lax.optimization_barrier((first, met))
    totals = totals + met
    met = across(totals, far)
    second, met = lax.optimization_barrier((second, met))
    totals = totals + met
    back = jnp.concatenate([first, second], axis=0).reshape(replicas, share, width)
    back, totals = lax.optimization_barrier((back, totals))
    arrived = exchanged(back, "rep")

    own_grad = lax.dynamic_slice_in_dim(grad_pre, replica * share, share, 0)
    self_term = lax.dot_general(
        own_grad, weight_self, CONTRACT_COLUMNS, preferred_element_type=f32
    )
    own_rows = (self_term + added([arrived[i] for i in range(replicas)])).astype(bf16)
    everything = copies_from_all(
        jnp.concatenate([own_rows, totals[: 2 * part].astype(bf16)], axis=0), "rep"
    )
    grad_features = everything[:, :share].reshape(rows, width)
    grad_self = everything[:, share : share + part].reshape(width, width).astype(f32)
    grad_neighbor = everything[:, share + part :].reshape(width, width).astype(f32)
    grad_bias = totals[2 * part]
    return (activations, grad_features, grad_self, grad_neighbor, grad_bias)


def solution(mesh):
    placed = (
        P("blk", None),
        P(),
        P(),
        P(),
        P("blk", "rep", None),
        P("blk", "rep", None),
        P("blk", "rep", None),
        P("blk", "rep"),
        P(("blk", "rep"), None, None),
        P("blk", None),
    )
    return jax.shard_map(
        on_device,
        mesh=mesh,
        in_specs=placed,
        out_specs=(P("blk", None), P("blk", None), P(), P(), P()),
        check_vma=False,
    )
```

```python
import functools

import jax
import jax.numpy as jnp
from jax import lax
from jax.experimental import pallas as pl
from jax.experimental.pallas import tpu as pltpu
from jax.sharding import PartitionSpec as P

BOTH = ("blk", "rep")
CONTRACT_ROWS = (((0,), (0,)), ((), ()))
CONTRACT_COLUMNS = (((1,), (1,)), ((), ()))


def permuted(array, target):
    groups, replicas = lax.axis_size("blk"), lax.axis_size("rep")
    pairs = []
    for g in range(groups):
        for r in range(replicas):
            to_g, to_r = target(g, r)
            pairs.append((g * replicas + r, to_g % groups * replicas + to_r % replicas))
    return lax.ppermute(array, BOTH, pairs)


def build_kernel(row_ref, column_ref, value_ref, count_ref, table_ref, *refs):
    out_refs, total_ref = refs[:-1], refs[-1]
    blocks = total_ref.shape[0]
    for step, out_ref in enumerate(out_refs):
        total_ref[...] = jnp.zeros_like(total_ref)

        def add_tile(slot, unused, step=step):
            row = row_ref[step, slot]
            column = column_ref[step, slot]
            value = value_ref[step, slot]
            total_ref[row, column] += table_ref[value].astype(jnp.float32)
            return unused

        lax.fori_loop(0, count_ref[step], add_tile, 0)
        for row in range(blocks):
            for column in range(blocks):
                out_ref[row * 128 : row * 128 + 128, column * 128 : column * 128 + 128] = total_ref[
                    row, column
                ].astype(out_ref.dtype)


def dense_blocks(rows, columns, values, counts, table, blocks):
    steps = rows.shape[0]
    tile = table.shape[1]
    side = blocks * tile
    whole = pl.BlockSpec(memory_space=pltpu.VMEM)
    scalars = pl.BlockSpec(memory_space=pltpu.SMEM)
    return pl.pallas_call(
        build_kernel,
        out_shape=[jax.ShapeDtypeStruct((side, side), table.dtype)] * steps,
        in_specs=[scalars] * 4 + [whole],
        out_specs=[whole] * steps,
        scratch_shapes=[pltpu.VMEM((blocks, blocks, tile, tile), jnp.float32)],
        compiler_params=pltpu.CompilerParams(vmem_limit_bytes=24 << 20),
        cost_estimate=pl.CostEstimate(flops=20_000_000, bytes_accessed=24 << 20, transcendentals=0),
    )(rows, columns, values, counts, table)


def exchanged(blocks, axis):
    return lax.all_to_all(blocks, axis, 0, 0, tiled=True)


def copies_from_all(array, axis):
    length = lax.axis_size(axis)
    return exchanged(jnp.broadcast_to(array[None], (length, *array.shape)), axis)


def added(arrays):
    total = arrays[0].astype(jnp.float32)
    for array in arrays[1:]:
        total = total + array.astype(jnp.float32)
    return total


def on_device(
    features,
    weight_self,
    weight_neighbor,
    bias_vector,
    tile_row,
    tile_column,
    tile_value,
    tile_count,
    tile_table,
    cotangent,
):
    groups = lax.axis_size("blk")
    replicas = lax.axis_size("rep")
    steps = groups // replicas
    replica = lax.axis_index("rep")
    rows, width = features.shape
    tile = tile_table.shape[1]
    share = rows // replicas
    half = rows // 2
    bf16, f32 = jnp.bfloat16, jnp.float32

    first = permuted(features[:half], lambda g, r: (g + steps * r + 1, r))
    second = permuted(features[half:], lambda g, r: (g + steps * (r ^ 2) + 1, r ^ 2))
    matrices = dense_blocks(
        tile_row[0], tile_column[0], tile_value[0], tile_count[0], tile_table, rows // tile
    )
    first, second, matrices = lax.optimization_barrier((first, second, matrices))
    panel_1 = jnp.concatenate([first, second], axis=0)
    panel_2 = permuted(panel_1, lambda g, r: (g + 1, r))
    panel_0 = permuted(panel_1, lambda g, r: (g - 1, r))
    panel_3 = permuted(panel_2, lambda g, r: (g + 1, r))

    partial = jnp.dot(matrices[1], panel_1, preferred_element_type=f32)
    partial += jnp.dot(matrices[2], panel_2, preferred_element_type=f32)
    partial += jnp.dot(matrices[0], panel_0, preferred_element_type=f32)
    partial += jnp.dot(matrices[3], panel_3, preferred_element_type=f32)

    arrived = exchanged(partial.astype(bf16).reshape(replicas, share, width), "rep")
    own_aggregate = added([arrived[i] for i in range(replicas)]).astype(bf16)
    aggregate = copies_from_all(own_aggregate, "rep").reshape(rows, width)

    pre = jnp.dot(features, weight_self, preferred_element_type=f32)
    pre = pre + jnp.dot(aggregate, weight_neighbor, preferred_element_type=f32) + bias_vector
    sigmoid_pre = jax.nn.sigmoid(pre)
    activations = (pre * sigmoid_pre).astype(bf16)
    derivative = sigmoid_pre * (1.0 + pre * (1.0 - sigmoid_pre))
    grad_pre = (cotangent.astype(f32) * derivative).astype(bf16)
    sent_back = lax.dot_general(
        grad_pre, weight_neighbor, CONTRACT_COLUMNS, preferred_element_type=f32
    ).astype(bf16)

    def pushed(step):
        return lax.dot_general(
            matrices[step], sent_back, CONTRACT_ROWS, preferred_element_type=f32
        )

    push_3 = pushed(3).astype(bf16)
    push_0 = pushed(0).astype(bf16)
    sum_3 = permuted(push_3, lambda g, r: (g - 1, r))
    sum_0 = permuted(push_0, lambda g, r: (g + 1, r))
    grad_pre, push_0, push_3 = lax.optimization_barrier((grad_pre, push_0, push_3))

    part = width // replicas
    grad_self = lax.dot_general(features, grad_pre, CONTRACT_ROWS, preferred_element_type=f32)
    grad_neighbor = lax.dot_general(aggregate, grad_pre, CONTRACT_ROWS, preferred_element_type=f32)
    grad_offset = jnp.sum(grad_pre.astype(f32), axis=0)
    totals = jnp.concatenate(
        [
            lax.dynamic_slice_in_dim(grad_self, replica * part, part, 0),
            lax.dynamic_slice_in_dim(grad_neighbor, replica * part, part, 0),
            jnp.pad(grad_offset[None], ((0, 7), (0, 0))),
        ],
        axis=0,
    )
    def across(array, bit):
        return permuted(array, lambda g, r: (g ^ bit, r))

    core, near, middle, far, side = [1 << n for n in range(groups.bit_length() - 1)]
    totals = totals + across(totals, core)
    sum_3, totals = lax.optimization_barrier((sum_3, totals))
    sum_2 = permuted((pushed(2) + sum_3.astype(f32)).astype(bf16), lambda g, r: (g - 1, r))
    totals = totals + across(totals, side)
    sum_2, sum_0, totals = lax.optimization_barrier((sum_2, sum_0, totals))
    sum_1 = (pushed(1) + added([sum_0, sum_2])).astype(bf16)

    cut = rows * 5 // 8
    first = permuted(sum_1[:cut], lambda g, r: (g - steps * r - 1, r))
    second = permuted(sum_1[cut:], lambda g, r: (g, r ^ 2))
    second, totals = lax.optimization_barrier((second, totals))
    second = permuted(second, lambda g, r: (g - steps * (r ^ 2) - 1, r))
    totals = totals + across(totals, near)
    first, totals = lax.optimization_barrier((first, totals))
    totals = totals + across(totals, middle)
    second, totals = lax.optimization_barrier((second, totals))
    last = across(totals, far)
    back = jnp.concatenate([first, second], axis=0).reshape(replicas, share, width)
    arrived = exchanged(back, "rep")
    last, arrived = lax.optimization_barrier((last, arrived))
    totals = totals + last

    own_grad = lax.dynamic_slice_in_dim(grad_pre, replica * share, share, 0)
    self_term = lax.dot_general(
        own_grad, weight_self, CONTRACT_COLUMNS, preferred_element_type=f32
    )
    own_rows = (self_term + added([arrived[i] for i in range(replicas)])).astype(bf16)
    everything = copies_from_all(
        jnp.concatenate([own_rows, totals[: 2 * part].astype(bf16)], axis=0), "rep"
    )
    grad_features = everything[:, :share].reshape(rows, width)
    grad_self = everything[:, share : share + part].reshape(width, width).astype(f32)
    grad_neighbor = everything[:, share + part :].reshape(width, width).astype(f32)
    grad_bias = totals[2 * part]
    return (activations, grad_features, grad_self, grad_neighbor, grad_bias)


def solution(mesh):
    placed = (
        P("blk", None),
        P(),
        P(),
        P(),
        P("blk", "rep", None),
        P("blk", "rep", None),
        P("blk", "rep", None),
        P("blk", "rep"),
        P(("blk", "rep"), None, None),
        P("blk", None),
    )
    return jax.shard_map(
        on_device,
        mesh=mesh,
        in_specs=placed,
        out_specs=(P("blk", None), P("blk", None), P(), P(), P()),
        check_vma=False,
    )
```

```python
import functools

import jax
import jax.numpy as jnp
from jax import lax
from jax.experimental import pallas as pl
from jax.experimental.pallas import tpu as pltpu
from jax.sharding import PartitionSpec as P

BOTH = ("blk", "rep")
CONTRACT_ROWS = (((0,), (0,)), ((), ()))
CONTRACT_COLUMNS = (((1,), (1,)), ((), ()))


def permuted(array, target):
    groups, replicas = lax.axis_size("blk"), lax.axis_size("rep")
    pairs = []
    for g in range(groups):
        for r in range(replicas):
            to_g, to_r = target(g, r)
            pairs.append((g * replicas + r, to_g % groups * replicas + to_r % replicas))
    return lax.ppermute(array, BOTH, pairs)


def build_kernel(row_ref, column_ref, value_ref, count_ref, table_ref, *refs):
    out_refs, total_ref = refs[:-1], refs[-1]
    blocks = total_ref.shape[0]
    for step, out_ref in enumerate(out_refs):
        total_ref[...] = jnp.zeros_like(total_ref)

        def add_tile(slot, unused, step=step):
            row = row_ref[step, slot]
            column = column_ref[step, slot]
            value = value_ref[step, slot]
            total_ref[row, column] += table_ref[value].astype(jnp.float32)
            return unused

        lax.fori_loop(0, count_ref[step], add_tile, 0)
        for row in range(blocks):
            for column in range(blocks):
                out_ref[row * 128 : row * 128 + 128, column * 128 : column * 128 + 128] = total_ref[
                    row, column
                ].astype(out_ref.dtype)


def dense_blocks(rows, columns, values, counts, table, blocks):
    steps = rows.shape[0]
    tile = table.shape[1]
    side = blocks * tile
    whole = pl.BlockSpec(memory_space=pltpu.VMEM)
    scalars = pl.BlockSpec(memory_space=pltpu.SMEM)
    return pl.pallas_call(
        build_kernel,
        out_shape=[jax.ShapeDtypeStruct((side, side), table.dtype)] * steps,
        in_specs=[scalars] * 4 + [whole],
        out_specs=[whole] * steps,
        scratch_shapes=[pltpu.VMEM((blocks, blocks, tile, tile), jnp.float32)],
        compiler_params=pltpu.CompilerParams(vmem_limit_bytes=24 << 20),
        cost_estimate=pl.CostEstimate(flops=20_000_000, bytes_accessed=24 << 20, transcendentals=0),
    )(rows, columns, values, counts, table)


def exchanged(blocks, axis):
    return lax.all_to_all(blocks, axis, 0, 0, tiled=True)


def copies_from_all(array, axis):
    length = lax.axis_size(axis)
    return exchanged(jnp.broadcast_to(array[None], (length, *array.shape)), axis)


def added(arrays):
    total = arrays[0].astype(jnp.float32)
    for array in arrays[1:]:
        total = total + array.astype(jnp.float32)
    return total


def on_device(
    features,
    weight_self,
    weight_neighbor,
    bias_vector,
    tile_row,
    tile_column,
    tile_value,
    tile_count,
    tile_table,
    cotangent,
):
    groups = lax.axis_size("blk")
    replicas = lax.axis_size("rep")
    steps = groups // replicas
    replica = lax.axis_index("rep")
    rows, width = features.shape
    tile = tile_table.shape[1]
    share = rows // replicas
    half = rows // 2
    bf16, f32 = jnp.bfloat16, jnp.float32

    first = permuted(features[:half], lambda g, r: (g + steps * r + 1, r))
    second = permuted(features[half:], lambda g, r: (g + steps * (r ^ 2) + 1, r ^ 2))
    matrices = dense_blocks(
        tile_row[0], tile_column[0], tile_value[0], tile_count[0], tile_table, rows // tile
    )
    first, second, matrices = lax.optimization_barrier((first, second, matrices))
    panel_1 = jnp.concatenate([first, second], axis=0)
    panel_2 = permuted(panel_1, lambda g, r: (g + 1, r))
    panel_0 = permuted(panel_1, lambda g, r: (g - 1, r))
    panel_3 = permuted(panel_2, lambda g, r: (g + 1, r))

    partial = jnp.dot(matrices[1], panel_1, preferred_element_type=f32)
    partial += jnp.dot(matrices[2], panel_2, preferred_element_type=f32)
    partial += jnp.dot(matrices[0], panel_0, preferred_element_type=f32)
    partial += jnp.dot(matrices[3], panel_3, preferred_element_type=f32)

    arrived = exchanged(partial.astype(bf16).reshape(replicas, share, width), "rep")
    own_aggregate = added([arrived[i] for i in range(replicas)]).astype(bf16)
    aggregate = copies_from_all(own_aggregate, "rep").reshape(rows, width)

    pre = jnp.dot(features, weight_self, preferred_element_type=f32)
    pre = pre + jnp.dot(aggregate, weight_neighbor, preferred_element_type=f32) + bias_vector
    sigmoid_pre = jax.nn.sigmoid(pre)
    activations = (pre * sigmoid_pre).astype(bf16)
    derivative = sigmoid_pre * (1.0 + pre * (1.0 - sigmoid_pre))
    grad_pre = (cotangent.astype(f32) * derivative).astype(bf16)
    sent_back = lax.dot_general(
        grad_pre, weight_neighbor, CONTRACT_COLUMNS, preferred_element_type=f32
    ).astype(bf16)

    def pushed(step):
        return lax.dot_general(
            matrices[step], sent_back, CONTRACT_ROWS, preferred_element_type=f32
        )

    push_3 = pushed(3).astype(bf16)
    sent_back, push_3 = lax.optimization_barrier((sent_back, push_3))
    push_0 = pushed(0).astype(bf16)
    sum_3 = permuted(push_3, lambda g, r: (g - 1, r))
    sum_0 = permuted(push_0, lambda g, r: (g + 1, r))
    grad_pre, push_0, push_3 = lax.optimization_barrier((grad_pre, push_0, push_3))

    part = width // replicas
    grad_self = lax.dot_general(features, grad_pre, CONTRACT_ROWS, preferred_element_type=f32)
    grad_neighbor = lax.dot_general(aggregate, grad_pre, CONTRACT_ROWS, preferred_element_type=f32)
    grad_offset = jnp.sum(grad_pre.astype(f32), axis=0)
    totals = jnp.concatenate(
        [
            lax.dynamic_slice_in_dim(grad_self, replica * part, part, 0),
            lax.dynamic_slice_in_dim(grad_neighbor, replica * part, part, 0),
            jnp.pad(grad_offset[None], ((0, 7), (0, 0))),
        ],
        axis=0,
    )
    def across(array, bit):
        return permuted(array, lambda g, r: (g ^ bit, r))

    core, near, middle, far, side = [1 << n for n in range(groups.bit_length() - 1)]
    totals = totals + across(totals, core)
    totals = totals + across(totals, side)
    sum_3, totals = lax.optimization_barrier((sum_3, totals))
    sum_2 = permuted((pushed(2) + sum_3.astype(f32)).astype(bf16), lambda g, r: (g - 1, r))
    totals = totals + across(totals, near)
    sum_2, sum_0, totals = lax.optimization_barrier((sum_2, sum_0, totals))
    sum_1 = (pushed(1) + added([sum_0, sum_2])).astype(bf16)

    cut = rows * 5 // 8
    first = permuted(sum_1[:cut], lambda g, r: (g - steps * r - 1, r))
    second = permuted(sum_1[cut:], lambda g, r: (g, r ^ 2))
    second, totals = lax.optimization_barrier((second, totals))
    second = permuted(second, lambda g, r: (g - steps * (r ^ 2) - 1, r))
    totals = totals + across(totals, middle)
    first, totals = lax.optimization_barrier((first, totals))
    totals = totals + across(totals, far)
    second, totals = lax.optimization_barrier((second, totals))
    back = jnp.concatenate([first, second], axis=0).reshape(replicas, share, width)
    arrived = exchanged(back, "rep")

    own_grad = lax.dynamic_slice_in_dim(grad_pre, replica * share, share, 0)
    self_term = lax.dot_general(
        own_grad, weight_self, CONTRACT_COLUMNS, preferred_element_type=f32
    )
    own_rows = (self_term + added([arrived[i] for i in range(replicas)])).astype(bf16)
    everything = copies_from_all(
        jnp.concatenate([own_rows, totals[: 2 * part].astype(bf16)], axis=0), "rep"
    )
    grad_features = everything[:, :share].reshape(rows, width)
    grad_self = everything[:, share : share + part].reshape(width, width).astype(f32)
    grad_neighbor = everything[:, share + part :].reshape(width, width).astype(f32)
    grad_bias = totals[2 * part]
    return (activations, grad_features, grad_self, grad_neighbor, grad_bias)


def solution(mesh):
    placed = (
        P("blk", None),
        P(),
        P(),
        P(),
        P("blk", "rep", None),
        P("blk", "rep", None),
        P("blk", "rep", None),
        P("blk", "rep"),
        P(("blk", "rep"), None, None),
        P("blk", None),
    )
    return jax.shard_map(
        on_device,
        mesh=mesh,
        in_specs=placed,
        out_specs=(P("blk", None), P("blk", None), P(), P(), P()),
        check_vma=False,
    )
```

```python
import functools

import jax
import jax.numpy as jnp
from jax import lax
from jax.experimental import pallas as pl
from jax.experimental.pallas import tpu as pltpu
from jax.sharding import PartitionSpec as P

BOTH = ("blk", "rep")
CONTRACT_ROWS = (((0,), (0,)), ((), ()))
CONTRACT_COLUMNS = (((1,), (1,)), ((), ()))


def permuted(array, target):
    groups, replicas = lax.axis_size("blk"), lax.axis_size("rep")
    pairs = []
    for g in range(groups):
        for r in range(replicas):
            to_g, to_r = target(g, r)
            pairs.append((g * replicas + r, to_g % groups * replicas + to_r % replicas))
    return lax.ppermute(array, BOTH, pairs)


def build_kernel(row_ref, column_ref, value_ref, count_ref, table_ref, *refs):
    out_refs, total_ref = refs[:-1], refs[-1]
    blocks = total_ref.shape[0]
    for step, out_ref in enumerate(out_refs):
        total_ref[...] = jnp.zeros_like(total_ref)

        def add_tile(slot, unused, step=step):
            row = row_ref[step, slot]
            column = column_ref[step, slot]
            value = value_ref[step, slot]
            total_ref[row, column] += table_ref[value].astype(jnp.float32)
            return unused

        lax.fori_loop(0, count_ref[step], add_tile, 0)
        for row in range(blocks):
            for column in range(blocks):
                out_ref[row * 128 : row * 128 + 128, column * 128 : column * 128 + 128] = total_ref[
                    row, column
                ].astype(out_ref.dtype)


def dense_blocks(rows, columns, values, counts, table, blocks):
    steps = rows.shape[0]
    tile = table.shape[1]
    side = blocks * tile
    whole = pl.BlockSpec(memory_space=pltpu.VMEM)
    scalars = pl.BlockSpec(memory_space=pltpu.SMEM)
    return pl.pallas_call(
        build_kernel,
        out_shape=[jax.ShapeDtypeStruct((side, side), table.dtype)] * steps,
        in_specs=[scalars] * 4 + [whole],
        out_specs=[whole] * steps,
        scratch_shapes=[pltpu.VMEM((blocks, blocks, tile, tile), jnp.float32)],
        compiler_params=pltpu.CompilerParams(vmem_limit_bytes=24 << 20),
        cost_estimate=pl.CostEstimate(flops=20_000_000, bytes_accessed=24 << 20, transcendentals=0),
    )(rows, columns, values, counts, table)


def exchanged(blocks, axis):
    return lax.all_to_all(blocks, axis, 0, 0, tiled=True)


def copies_from_all(array, axis):
    length = lax.axis_size(axis)
    return exchanged(jnp.broadcast_to(array[None], (length, *array.shape)), axis)


def added(arrays):
    total = arrays[0].astype(jnp.float32)
    for array in arrays[1:]:
        total = total + array.astype(jnp.float32)
    return total


def on_device(
    features,
    weight_self,
    weight_neighbor,
    bias_vector,
    tile_row,
    tile_column,
    tile_value,
    tile_count,
    tile_table,
    cotangent,
):
    groups = lax.axis_size("blk")
    replicas = lax.axis_size("rep")
    steps = groups // replicas
    replica = lax.axis_index("rep")
    rows, width = features.shape
    tile = tile_table.shape[1]
    share = rows // replicas
    half = rows // 2
    bf16, f32 = jnp.bfloat16, jnp.float32

    first = permuted(features[:half], lambda g, r: (g + steps * r + 1, r))
    second = permuted(features[half:], lambda g, r: (g + steps * (r ^ 2) + 1, r ^ 2))
    matrices = dense_blocks(
        tile_row[0], tile_column[0], tile_value[0], tile_count[0], tile_table, rows // tile
    )
    first, second, matrices = lax.optimization_barrier((first, second, matrices))
    panel_1 = jnp.concatenate([first, second], axis=0)
    panel_2 = permuted(panel_1, lambda g, r: (g + 1, r))
    panel_0 = permuted(panel_1, lambda g, r: (g - 1, r))
    panel_3 = permuted(panel_2, lambda g, r: (g + 1, r))

    partial = jnp.dot(matrices[1], panel_1, preferred_element_type=f32)
    partial += jnp.dot(matrices[2], panel_2, preferred_element_type=f32)
    partial += jnp.dot(matrices[0], panel_0, preferred_element_type=f32)
    partial += jnp.dot(matrices[3], panel_3, preferred_element_type=f32)

    arrived = exchanged(partial.astype(bf16).reshape(replicas, share, width), "rep")
    own_aggregate = added([arrived[i] for i in range(replicas)]).astype(bf16)
    aggregate = copies_from_all(own_aggregate, "rep").reshape(rows, width)

    pre = jnp.dot(features, weight_self, preferred_element_type=f32)
    pre = pre + jnp.dot(aggregate, weight_neighbor, preferred_element_type=f32) + bias_vector
    sigmoid_pre = jax.nn.sigmoid(pre)
    activations = (pre * sigmoid_pre).astype(bf16)
    derivative = sigmoid_pre * (1.0 + pre * (1.0 - sigmoid_pre))
    grad_pre = (cotangent.astype(f32) * derivative).astype(bf16)
    sent_back = lax.dot_general(
        grad_pre, weight_neighbor, CONTRACT_COLUMNS, preferred_element_type=f32
    ).astype(bf16)

    def pushed(step):
        return lax.dot_general(
            matrices[step], sent_back, CONTRACT_ROWS, preferred_element_type=f32
        )

    push_3 = pushed(3).astype(bf16)
    sent_back, push_3 = lax.optimization_barrier((sent_back, push_3))
    push_0 = pushed(0).astype(bf16)
    sum_3 = permuted(push_3, lambda g, r: (g - 1, r))
    sum_0 = permuted(push_0, lambda g, r: (g + 1, r))
    grad_pre, push_0, push_3 = lax.optimization_barrier((grad_pre, push_0, push_3))

    part = width // replicas
    grad_self = lax.dot_general(features, grad_pre, CONTRACT_ROWS, preferred_element_type=f32)
    grad_neighbor = lax.dot_general(aggregate, grad_pre, CONTRACT_ROWS, preferred_element_type=f32)
    grad_offset = jnp.sum(grad_pre.astype(f32), axis=0)
    totals = jnp.concatenate(
        [
            lax.dynamic_slice_in_dim(grad_self, replica * part, part, 0),
            lax.dynamic_slice_in_dim(grad_neighbor, replica * part, part, 0),
            jnp.pad(grad_offset[None], ((0, 7), (0, 0))),
        ],
        axis=0,
    )
    def across(array, bit):
        return permuted(array, lambda g, r: (g ^ bit, r))

    core, near, middle, far, side = [1 << n for n in range(groups.bit_length() - 1)]
    totals = totals + across(totals, core)
    totals = totals + across(totals, side)
    sum_3, totals = lax.optimization_barrier((sum_3, totals))
    sum_2 = permuted((pushed(2) + sum_3.astype(f32)).astype(bf16), lambda g, r: (g - 1, r))
    totals = totals + across(totals, near)
    sum_2, sum_0, totals = lax.optimization_barrier((sum_2, sum_0, totals))
    sum_1 = (pushed(1) + added([sum_0, sum_2])).astype(bf16)

    cut = rows * 5 // 8
    first = permuted(sum_1[:cut], lambda g, r: (g - steps * r - 1, r))
    second = permuted(sum_1[cut:], lambda g, r: (g, r ^ 2))
    second, totals = lax.optimization_barrier((second, totals))
    second = permuted(second, lambda g, r: (g - steps * (r ^ 2) - 1, r))
    met = [across(totals, bits) for bits in (middle, far, middle | far)]
    totals = (totals + met[0]) + (met[1] + met[2])
    second, totals = lax.optimization_barrier((second, totals))
    back = jnp.concatenate([first, second], axis=0).reshape(replicas, share, width)
    arrived = exchanged(back, "rep")

    own_grad = lax.dynamic_slice_in_dim(grad_pre, replica * share, share, 0)
    self_term = lax.dot_general(
        own_grad, weight_self, CONTRACT_COLUMNS, preferred_element_type=f32
    )
    own_rows = (self_term + added([arrived[i] for i in range(replicas)])).astype(bf16)
    everything = copies_from_all(
        jnp.concatenate([own_rows, totals[: 2 * part].astype(bf16)], axis=0), "rep"
    )
    grad_features = everything[:, :share].reshape(rows, width)
    grad_self = everything[:, share : share + part].reshape(width, width).astype(f32)
    grad_neighbor = everything[:, share + part :].reshape(width, width).astype(f32)
    grad_bias = totals[2 * part]
    return (activations, grad_features, grad_self, grad_neighbor, grad_bias)


def solution(mesh):
    placed = (
        P("blk", None),
        P(),
        P(),
        P(),
        P("blk", "rep", None),
        P("blk", "rep", None),
        P("blk", "rep", None),
        P("blk", "rep"),
        P(("blk", "rep"), None, None),
        P("blk", None),
    )
    return jax.shard_map(
        on_device,
        mesh=mesh,
        in_specs=placed,
        out_specs=(P("blk", None), P("blk", None), P(), P(), P()),
        check_vma=False,
    )
```

```python
import functools

import jax
import jax.numpy as jnp
from jax import lax
from jax.experimental import pallas as pl
from jax.experimental.pallas import tpu as pltpu
from jax.sharding import PartitionSpec as P

BOTH = ("blk", "rep")
CONTRACT_ROWS = (((0,), (0,)), ((), ()))
CONTRACT_COLUMNS = (((1,), (1,)), ((), ()))


def permuted(array, target):
    groups, replicas = lax.axis_size("blk"), lax.axis_size("rep")
    pairs = []
    for g in range(groups):
        for r in range(replicas):
            to_g, to_r = target(g, r)
            pairs.append((g * replicas + r, to_g % groups * replicas + to_r % replicas))
    return lax.ppermute(array, BOTH, pairs)


def build_kernel(row_ref, column_ref, value_ref, count_ref, table_ref, *refs):
    out_refs, total_ref = refs[:-1], refs[-1]
    blocks = total_ref.shape[0]
    for step, out_ref in enumerate(out_refs):
        total_ref[...] = jnp.zeros_like(total_ref)

        def add_tile(slot, unused, step=step):
            row = row_ref[step, slot]
            column = column_ref[step, slot]
            value = value_ref[step, slot]
            total_ref[row, column] += table_ref[value].astype(jnp.float32)
            return unused

        lax.fori_loop(0, count_ref[step], add_tile, 0)
        for row in range(blocks):
            for column in range(blocks):
                out_ref[row * 128 : row * 128 + 128, column * 128 : column * 128 + 128] = total_ref[
                    row, column
                ].astype(out_ref.dtype)


def dense_blocks(rows, columns, values, counts, table, blocks):
    steps = rows.shape[0]
    tile = table.shape[1]
    side = blocks * tile
    whole = pl.BlockSpec(memory_space=pltpu.VMEM)
    scalars = pl.BlockSpec(memory_space=pltpu.SMEM)
    return pl.pallas_call(
        build_kernel,
        out_shape=[jax.ShapeDtypeStruct((side, side), table.dtype)] * steps,
        in_specs=[scalars] * 4 + [whole],
        out_specs=[whole] * steps,
        scratch_shapes=[pltpu.VMEM((blocks, blocks, tile, tile), jnp.float32)],
        compiler_params=pltpu.CompilerParams(vmem_limit_bytes=24 << 20),
        cost_estimate=pl.CostEstimate(flops=20_000_000, bytes_accessed=24 << 20, transcendentals=0),
    )(rows, columns, values, counts, table)


def exchanged(blocks, axis):
    return lax.all_to_all(blocks, axis, 0, 0, tiled=True)


def copies_from_all(array, axis):
    length = lax.axis_size(axis)
    return exchanged(jnp.broadcast_to(array[None], (length, *array.shape)), axis)


def added(arrays):
    total = arrays[0].astype(jnp.float32)
    for array in arrays[1:]:
        total = total + array.astype(jnp.float32)
    return total


def on_device(
    features,
    weight_self,
    weight_neighbor,
    bias_vector,
    tile_row,
    tile_column,
    tile_value,
    tile_count,
    tile_table,
    cotangent,
):
    groups = lax.axis_size("blk")
    replicas = lax.axis_size("rep")
    steps = groups // replicas
    replica = lax.axis_index("rep")
    rows, width = features.shape
    tile = tile_table.shape[1]
    share = rows // replicas
    half = rows // 2
    bf16, f32 = jnp.bfloat16, jnp.float32

    first = permuted(features[:half], lambda g, r: (g + steps * r + 1, r))
    second = permuted(features[half:], lambda g, r: (g + steps * (r ^ 2) + 1, r ^ 2))
    matrices = dense_blocks(
        tile_row[0], tile_column[0], tile_value[0], tile_count[0], tile_table, rows // tile
    )
    first, second, matrices = lax.optimization_barrier((first, second, matrices))
    panel_1 = jnp.concatenate([first, second], axis=0)
    panel_2 = permuted(panel_1, lambda g, r: (g + 1, r))
    panel_0 = permuted(panel_1, lambda g, r: (g - 1, r))
    panel_3 = permuted(panel_2, lambda g, r: (g + 1, r))

    partial = jnp.dot(matrices[1], panel_1, preferred_element_type=f32)
    partial += jnp.dot(matrices[2], panel_2, preferred_element_type=f32)
    partial += jnp.dot(matrices[0], panel_0, preferred_element_type=f32)
    partial += jnp.dot(matrices[3], panel_3, preferred_element_type=f32)

    arrived = exchanged(partial.astype(bf16).reshape(replicas, share, width), "rep")
    own_aggregate = added([arrived[i] for i in range(replicas)]).astype(bf16)
    aggregate = copies_from_all(own_aggregate, "rep").reshape(rows, width)

    pre = jnp.dot(features, weight_self, preferred_element_type=f32)
    pre = pre + jnp.dot(aggregate, weight_neighbor, preferred_element_type=f32) + bias_vector
    sigmoid_pre = jax.nn.sigmoid(pre)
    activations = (pre * sigmoid_pre).astype(bf16)
    derivative = sigmoid_pre * (1.0 + pre * (1.0 - sigmoid_pre))
    grad_pre = (cotangent.astype(f32) * derivative).astype(bf16)
    sent_back = lax.dot_general(
        grad_pre, weight_neighbor, CONTRACT_COLUMNS, preferred_element_type=f32
    ).astype(bf16)

    def pushed(step):
        return lax.dot_general(
            matrices[step], sent_back, CONTRACT_ROWS, preferred_element_type=f32
        )

    push_3 = pushed(3).astype(bf16)
    sent_back, push_3 = lax.optimization_barrier((sent_back, push_3))
    push_0 = pushed(0).astype(bf16)
    sum_3 = permuted(push_3, lambda g, r: (g - 1, r))
    sum_0 = permuted(push_0, lambda g, r: (g + 1, r))
    grad_pre, push_0, push_3 = lax.optimization_barrier((grad_pre, push_0, push_3))

    part = width // replicas
    grad_self = lax.dot_general(features, grad_pre, CONTRACT_ROWS, preferred_element_type=f32)
    grad_neighbor = lax.dot_general(aggregate, grad_pre, CONTRACT_ROWS, preferred_element_type=f32)
    grad_offset = jnp.sum(grad_pre.astype(f32), axis=0)
    totals = jnp.concatenate(
        [
            lax.dynamic_slice_in_dim(grad_self, replica * part, part, 0),
            lax.dynamic_slice_in_dim(grad_neighbor, replica * part, part, 0),
            jnp.pad(grad_offset[None], ((0, 7), (0, 0))),
        ],
        axis=0,
    )
    def across(array, bit):
        return permuted(array, lambda g, r: (g ^ bit, r))

    core, near, middle, far, side = [1 << n for n in range(groups.bit_length() - 1)]
    totals = totals + across(totals, core)
    totals = totals + across(totals, side)
    sum_3, totals = lax.optimization_barrier((sum_3, totals))
    sum_2 = permuted((pushed(2) + sum_3.astype(f32)).astype(bf16), lambda g, r: (g - 1, r))
    totals = totals + across(totals, near)
    sum_2, sum_0, totals = lax.optimization_barrier((sum_2, sum_0, totals))
    sum_1 = (pushed(1) + added([sum_0, sum_2])).astype(bf16)

    cut = rows * 5 // 8
    first = permuted(sum_1[:cut], lambda g, r: (g - steps * r - 1, r))
    second = permuted(sum_1[cut:], lambda g, r: (g, r ^ 2))
    second, totals = lax.optimization_barrier((second, totals))
    second = permuted(second, lambda g, r: (g - steps * (r ^ 2) - 1, r))
    first, second, totals = lax.optimization_barrier((first, second, totals))
    met = [across(totals, bits) for bits in (middle, far, middle | far)]
    back = jnp.concatenate([first, second], axis=0).reshape(replicas, share, width)
    arrived = exchanged(back, "rep")
    *met, arrived = lax.optimization_barrier((*met, arrived))
    totals = (totals + met[0]) + (met[1] + met[2])

    own_grad = lax.dynamic_slice_in_dim(grad_pre, replica * share, share, 0)
    self_term = lax.dot_general(
        own_grad, weight_self, CONTRACT_COLUMNS, preferred_element_type=f32
    )
    own_rows = (self_term + added([arrived[i] for i in range(replicas)])).astype(bf16)
    everything = copies_from_all(
        jnp.concatenate([own_rows, totals[: 2 * part].astype(bf16)], axis=0), "rep"
    )
    grad_features = everything[:, :share].reshape(rows, width)
    grad_self = everything[:, share : share + part].reshape(width, width).astype(f32)
    grad_neighbor = everything[:, share + part :].reshape(width, width).astype(f32)
    grad_bias = totals[2 * part]
    return (activations, grad_features, grad_self, grad_neighbor, grad_bias)


def solution(mesh):
    placed = (
        P("blk", None),
        P(),
        P(),
        P(),
        P("blk", "rep", None),
        P("blk", "rep", None),
        P("blk", "rep", None),
        P("blk", "rep"),
        P(("blk", "rep"), None, None),
        P("blk", None),
    )
    return jax.shard_map(
        on_device,
        mesh=mesh,
        in_specs=placed,
        out_specs=(P("blk", None), P("blk", None), P(), P(), P()),
        check_vma=False,
    )
```

```python
import functools

import jax
import jax.numpy as jnp
from jax import lax
from jax.experimental import pallas as pl
from jax.experimental.pallas import tpu as pltpu
from jax.sharding import PartitionSpec as P

BOTH = ("blk", "rep")
CONTRACT_ROWS = (((0,), (0,)), ((), ()))
CONTRACT_COLUMNS = (((1,), (1,)), ((), ()))


def permuted(array, target):
    groups, replicas = lax.axis_size("blk"), lax.axis_size("rep")
    pairs = []
    for g in range(groups):
        for r in range(replicas):
            to_g, to_r = target(g, r)
            pairs.append((g * replicas + r, to_g % groups * replicas + to_r % replicas))
    return lax.ppermute(array, BOTH, pairs)


def build_kernel(row_ref, column_ref, value_ref, count_ref, table_ref, *refs):
    out_refs, total_ref = refs[:-1], refs[-1]
    blocks = total_ref.shape[0]
    for step, out_ref in enumerate(out_refs):
        total_ref[...] = jnp.zeros_like(total_ref)

        def add_tile(slot, unused, step=step):
            row = row_ref[step, slot]
            column = column_ref[step, slot]
            value = value_ref[step, slot]
            total_ref[row, column] += table_ref[value].astype(jnp.float32)
            return unused

        lax.fori_loop(0, count_ref[step], add_tile, 0)
        for row in range(blocks):
            for column in range(blocks):
                out_ref[row * 128 : row * 128 + 128, column * 128 : column * 128 + 128] = total_ref[
                    row, column
                ].astype(out_ref.dtype)


def dense_blocks(rows, columns, values, counts, table, blocks):
    steps = rows.shape[0]
    tile = table.shape[1]
    side = blocks * tile
    whole = pl.BlockSpec(memory_space=pltpu.VMEM)
    scalars = pl.BlockSpec(memory_space=pltpu.SMEM)
    return pl.pallas_call(
        build_kernel,
        out_shape=[jax.ShapeDtypeStruct((side, side), table.dtype)] * steps,
        in_specs=[scalars] * 4 + [whole],
        out_specs=[whole] * steps,
        scratch_shapes=[pltpu.VMEM((blocks, blocks, tile, tile), jnp.float32)],
        compiler_params=pltpu.CompilerParams(vmem_limit_bytes=24 << 20),
        cost_estimate=pl.CostEstimate(flops=20_000_000, bytes_accessed=24 << 20, transcendentals=0),
    )(rows, columns, values, counts, table)


def exchanged(blocks, axis):
    return lax.all_to_all(blocks, axis, 0, 0, tiled=True)


def copies_from_all(array, axis):
    length = lax.axis_size(axis)
    return exchanged(jnp.broadcast_to(array[None], (length, *array.shape)), axis)


def added(arrays):
    total = arrays[0].astype(jnp.float32)
    for array in arrays[1:]:
        total = total + array.astype(jnp.float32)
    return total


def on_device(
    features,
    weight_self,
    weight_neighbor,
    bias_vector,
    tile_row,
    tile_column,
    tile_value,
    tile_count,
    tile_table,
    cotangent,
):
    groups = lax.axis_size("blk")
    replicas = lax.axis_size("rep")
    steps = groups // replicas
    replica = lax.axis_index("rep")
    rows, width = features.shape
    tile = tile_table.shape[1]
    share = rows // replicas
    half = rows // 2
    bf16, f32 = jnp.bfloat16, jnp.float32

    first = permuted(features[:half], lambda g, r: (g + steps * r + 1, r))
    second = permuted(features[half:], lambda g, r: (g + steps * (r ^ 2) + 1, r ^ 2))
    matrices = dense_blocks(
        tile_row[0], tile_column[0], tile_value[0], tile_count[0], tile_table, rows // tile
    )
    first, second, matrices = lax.optimization_barrier((first, second, matrices))
    panel_1 = jnp.concatenate([first, second], axis=0)
    panel_2 = permuted(panel_1, lambda g, r: (g + 1, r))
    panel_0 = permuted(panel_1, lambda g, r: (g - 1, r))
    panel_3 = permuted(panel_2, lambda g, r: (g + 1, r))

    partial = jnp.dot(matrices[1], panel_1, preferred_element_type=f32)
    partial += jnp.dot(matrices[2], panel_2, preferred_element_type=f32)
    partial += jnp.dot(matrices[0], panel_0, preferred_element_type=f32)
    partial += jnp.dot(matrices[3], panel_3, preferred_element_type=f32)

    arrived = exchanged(partial.astype(bf16).reshape(replicas, share, width), "rep")
    own_aggregate = added([arrived[i] for i in range(replicas)]).astype(bf16)
    aggregate = copies_from_all(own_aggregate, "rep").reshape(rows, width)

    pre = jnp.dot(features, weight_self, preferred_element_type=f32)
    pre = pre + jnp.dot(aggregate, weight_neighbor, preferred_element_type=f32) + bias_vector
    sigmoid_pre = jax.nn.sigmoid(pre)
    activations = (pre * sigmoid_pre).astype(bf16)
    derivative = sigmoid_pre * (1.0 + pre * (1.0 - sigmoid_pre))
    grad_pre = (cotangent.astype(f32) * derivative).astype(bf16)
    sent_back = lax.dot_general(
        grad_pre, weight_neighbor, CONTRACT_COLUMNS, preferred_element_type=f32
    ).astype(bf16)

    def pushed(step):
        return lax.dot_general(
            matrices[step], sent_back, CONTRACT_ROWS, preferred_element_type=f32
        )

    push_3 = pushed(3).astype(bf16)
    sent_back, push_3 = lax.optimization_barrier((sent_back, push_3))
    push_0 = pushed(0).astype(bf16)
    sum_3 = permuted(push_3, lambda g, r: (g - 1, r))
    sum_0 = permuted(push_0, lambda g, r: (g + 1, r))
    grad_pre, push_0, push_3 = lax.optimization_barrier((grad_pre, push_0, push_3))

    part = width // replicas
    grad_self = lax.dot_general(features, grad_pre, CONTRACT_ROWS, preferred_element_type=f32)
    grad_neighbor = lax.dot_general(aggregate, grad_pre, CONTRACT_ROWS, preferred_element_type=f32)
    grad_offset = jnp.sum(grad_pre.astype(f32), axis=0)
    totals = jnp.concatenate(
        [
            lax.dynamic_slice_in_dim(grad_self, replica * part, part, 0),
            lax.dynamic_slice_in_dim(grad_neighbor, replica * part, part, 0),
            jnp.pad(grad_offset[None], ((0, 7), (0, 0))),
        ],
        axis=0,
    )
    def across(array, bit):
        return permuted(array, lambda g, r: (g ^ bit, r))

    core, near, middle, far, side = [1 << n for n in range(groups.bit_length() - 1)]
    totals = totals + across(totals, core)
    totals = totals + across(totals, side)
    sum_3, totals = lax.optimization_barrier((sum_3, totals))
    sum_2 = permuted((pushed(2) + sum_3.astype(f32)).astype(bf16), lambda g, r: (g - 1, r))
    totals = totals + across(totals, near)
    sum_2, sum_0, totals = lax.optimization_barrier((sum_2, sum_0, totals))
    sum_1 = (pushed(1) + added([sum_0, sum_2])).astype(bf16)

    cut = rows * 5 // 8
    first = permuted(sum_1[:cut], lambda g, r: (g - steps * r - 1, r))
    second = permuted(sum_1[cut:], lambda g, r: (g, r ^ 2))
    second, totals = lax.optimization_barrier((second, totals))
    second = permuted(second, lambda g, r: (g - steps * (r ^ 2) - 1, r))
    totals = totals + across(totals, middle)
    first, second, totals = lax.optimization_barrier((first, second, totals))
    met = across(totals, far)
    back = jnp.concatenate([first, second], axis=0).reshape(replicas, share, width)
    arrived = exchanged(back, "rep")
    met, arrived = lax.optimization_barrier((met, arrived))
    totals = totals + met

    own_grad = lax.dynamic_slice_in_dim(grad_pre, replica * share, share, 0)
    self_term = lax.dot_general(
        own_grad, weight_self, CONTRACT_COLUMNS, preferred_element_type=f32
    )
    own_rows = (self_term + added([arrived[i] for i in range(replicas)])).astype(bf16)
    everything = copies_from_all(
        jnp.concatenate([own_rows, totals[: 2 * part].astype(bf16)], axis=0), "rep"
    )
    grad_features = everything[:, :share].reshape(rows, width)
    grad_self = everything[:, share : share + part].reshape(width, width).astype(f32)
    grad_neighbor = everything[:, share + part :].reshape(width, width).astype(f32)
    grad_bias = totals[2 * part]
    return (activations, grad_features, grad_self, grad_neighbor, grad_bias)


def solution(mesh):
    placed = (
        P("blk", None),
        P(),
        P(),
        P(),
        P("blk", "rep", None),
        P("blk", "rep", None),
        P("blk", "rep", None),
        P("blk", "rep"),
        P(("blk", "rep"), None, None),
        P("blk", None),
    )
    return jax.shard_map(
        on_device,
        mesh=mesh,
        in_specs=placed,
        out_specs=(P("blk", None), P("blk", None), P(), P(), P()),
        check_vma=False,
    )
```
